256 devices in a mesh: tensor: 64 (over x, z, core), dp: 4 (over y).
Axes of the slice: x: 4, y: 4, z: 8, core: 2. Of those that a mesh axis runs over, the one named last changes fastest.
Arguments:
- tokens: bfloat16 [512, 8192], P('tensor', 'dp'), may hold values from -6 to 6
- gate_weight: bfloat16 [8192, 26624], P('dp', 'tensor'), may hold values from -0.0625 to 0.0625
- up_weight: bfloat16 [8192, 26624], P('dp', 'tensor'), may hold values from -0.0625 to 0.0625
- down_weight: bfloat16 [26624, 8192], P('tensor', 'dp'), may hold values from -6 to 6
- inverse_hessian: bfloat16 [26624, 26624], P(('tensor', 'dp')), may hold values from -2 to 3, as said below
- damping: float32 [26624], replicated, may hold values from 1 to 2.5
- removed: int32 [512], replicated, may hold values from 0 to 26623, as said below
Outputs:
- pruned_down: bfloat16 [26112, 8192], P('tensor', 'dp')
- mixed: bfloat16 [512, 8192], P('tensor', 'dp')
The draws below stay inside these ranges and needn't reach their ends.
Inputs may be any that keep to these rules, and one draw needn't show every extreme that they name: `removed`: Strictly increasing. For every even t, the channels t * 416 to (t + 2) * 416 - 1 hold exactly 16 removed indices; the first half of them holds more than half of these when t // 2 is even and fewer when t // 2 is odd. Each aligned block of 104 channels holds at most 4 removed indices, and some block holds exactly 4. `inverse_hessian`: Symmetric; before its rounding to bfloat16 it is positive semidefinite.
All inputs are finite; a program needn't handle non-finite values.
Results may differ from the reference program's by a relative error of at most 0.0057.
Values may be sent and summed in bfloat16 or wider, within the bound.
A program may use at most 128 MiB of HBM per device.

```python
import math
import jax
import jax.numpy as jnp
from jax import lax

D = 8192
FF = 26624
REM_DEV = 2
REMOVED = 512
TOKENS = 512
N_TENSOR = 64
N_DP = 4


def draw_removed(key, part):
    key = jax.random.fold_in(key, 11)
    key_loads, key_pick, key_channels = jax.random.split(key, 3)
    pair_total = N_TENSOR // 2
    pair_quota = N_DP * REM_DEV
    skews = jax.random.randint(key_loads, (pair_total,), 1, pair_quota + 1)
    chosen = jax.random.randint(key_pick, (), 0, pair_total)
    skews = jnp.where(jnp.arange(pair_total) == chosen, pair_quota, skews)
    signs = 1 - 2 * (jnp.arange(pair_total) % 2)
    loads = pair_quota + signs * skews
    shard_loads = jnp.stack([loads, 2 * pair_quota - loads], axis=1).reshape(-1)
    device_loads = ((shard_loads[:, None] + jnp.arange(N_DP)[None, :]) // N_DP).reshape(-1)
    block_width = FF // (N_TENSOR * N_DP)
    scores = jax.random.randint(key_channels, (N_TENSOR * N_DP, block_width), 0, 1 << 20) * block_width
    scores = scores + jnp.arange(block_width)[None, :]
    ranking = jnp.argsort(jnp.argsort(scores, axis=1), axis=1)
    chosen_mask = (ranking < device_loads[:, None]).reshape(-1)
    return jnp.nonzero(chosen_mask, size=N_TENSOR * N_DP * REM_DEV)[0].astype(jnp.int32)


def draw_inverse_hessian(key, part):
    key = jax.random.fold_in(key, 23)
    key_place, key_scale, key_sign = jax.random.split(key, 3)
    spread = jax.random.uniform(key_place, (FF,), jnp.float32)
    places = spread
    scales = jnp.exp(jax.random.uniform(key_scale, (FF,), jnp.float32, math.log(0.5), math.log(2.0)))
    signs = (2 * jax.random.randint(key_sign, (FF,), 0, 2) - 1).astype(jnp.float32)
    distance = jnp.abs(places[:, None] - places[None, :])
    broad = 64.0 / REMOVED * jnp.exp(-0.5 * distance)
    narrow = 0.4 * (signs[:, None] * signs[None, :]) * jnp.exp(-distance * (REMOVED / 8.0))
    return (scales[:, None] * scales[None, :] * (broad + narrow)).astype(jnp.bfloat16)


def levels(stream_key, extent, cuts, low, high):
    gain = 1.0
    for position, parts in cuts:
        heights = jax.random.uniform(jax.random.fold_in(jax.random.fold_in(stream_key, 6), position), (parts,), jnp.float32, low / len(cuts), high / len(cuts))
        gain = gain * jnp.repeat(jnp.exp(heights), extent[position] // parts).reshape((-1,) + (1,) * (len(extent) - 1 - position))
    return gain


def gaussian(own_key, shape, scale, bound, pieces=(), kind=jnp.bfloat16):
    gain = levels(own_key, shape, pieces, -0.22, 0.18) if pieces else 1.0
    result = jax.random.normal(own_key, shape, jnp.float32) * scale * gain
    return jnp.minimum(jnp.maximum(result, -bound), bound).astype(kind)


def setup_inputs(seed: int = 0) -> dict:
    seeds = jax.random.split(jax.random.key(seed), 8)
    return {
        "tokens": gaussian(seeds[0], (TOKENS, D), 1.0, 6.0, ((0, 64), (1, 4))),
        "gate_weight": gaussian(seeds[1], (D, FF), D ** -0.5, 0.0625, ((0, 4), (1, 64))),
        "up_weight": gaussian(seeds[2], (D, FF), D ** -0.5, 0.0625, ((0, 4), (1, 64))),
        "down_weight": gaussian(seeds[3], (FF, D), 1.0, 6.0, ((0, 64), (1, 4))),
        "inverse_hessian": draw_inverse_hessian(jax.random.fold_in(seeds[7], 71), 0),
        "damping": jnp.clip(jnp.exp(jax.random.uniform(seeds[5], (FF,), jnp.float32, math.log(1.0), math.log(2.5))), 1.0, 2.5),
        "removed": draw_removed(jax.random.fold_in(seeds[7], 71), 0),
    }


def solve_pair(factor, right_side):
    forward = lax.linalg.triangular_solve(factor, right_side, left_side=True, lower=True)
    return lax.linalg.triangular_solve(factor, forward, left_side=True, lower=True, transpose_a=True)

def reference(tokens, gate_weight, up_weight, down_weight, inverse_hessian, damping, removed):
    flags = jnp.zeros((FF,), jnp.int32).at[removed].set(1)
    kept = jnp.nonzero(flags == 0, size=FF - REMOVED)[0].astype(jnp.int32)
    removed_rows = jnp.take(inverse_hessian, removed, axis=0).astype(jnp.float32)
    square = jnp.take(removed_rows, removed, axis=1) + jnp.diag(jnp.take(damping, removed))
    square = 0.5 * (square + square.T)
    factor = jnp.linalg.cholesky(square)
    coefficients = solve_pair(factor, jnp.take(removed_rows, kept, axis=1))
    lost_rows = jnp.take(down_weight, removed, axis=0).astype(jnp.float32)
    correction = lax.dot_general(coefficients, lost_rows, (((0,), (0,)), ((), ())), precision=lax.Precision.HIGHEST)
    pruned_down = (jnp.take(down_weight, kept, axis=0).astype(jnp.float32) - correction).astype(jnp.bfloat16)
    preact_gate = jnp.dot(tokens.astype(jnp.float32), jnp.take(gate_weight, kept, axis=1).astype(jnp.float32), preferred_element_type=jnp.float32)
    preact_up = jnp.dot(tokens.astype(jnp.float32), jnp.take(up_weight, kept, axis=1).astype(jnp.float32), preferred_element_type=jnp.float32)
    hidden = (jax.nn.silu(preact_gate) * preact_up).astype(jnp.bfloat16)
    mixed = jnp.dot(hidden.astype(jnp.float32), pruned_down.astype(jnp.float32), preferred_element_type=jnp.float32) * FF ** (-0.5)
    return (pruned_down, mixed.astype(jnp.bfloat16))
```

```python
import jax
import jax.numpy as jnp
from jax import lax
from jax.experimental import pallas as pl
from jax.experimental.pallas import tpu as pltpu
from jax.sharding import PartitionSpec as P

MESH = pl.DeviceIdType.MESH
BF = jnp.bfloat16
F32 = jnp.float32
NX, NZ, NY = 4, 8, 4
WIDTH = 416
BLOCK = 104
KEPT = 408
FF = 26624
REM = 512
STEPS = 8
VMEM_LIMIT = 52 * 1024 * 1024


def dot(a, b):
    return jnp.dot(a, b, preferred_element_type=F32)


def place():
    t = lax.axis_index("tensor")
    d = lax.axis_index("dp")
    return t // 16, (t // 2) % 8, t % 2, d


def at(x, z, c, d):
    return (x * 16 + z * 2 + c, d)


def remote(src, dst, send, recv, device):
    return pltpu.make_async_remote_copy(
        src_ref=src, dst_ref=dst, send_sem=send, recv_sem=recv, device_id=device, device_id_type=MESH
    )


def greet(devices):
    barrier = pltpu.get_barrier_semaphore()
    for device in devices:
        pl.semaphore_signal(barrier, inc=1, device_id=device, device_id_type=MESH)
    pl.semaphore_wait(barrier, len(devices))


def pair_indices(removed_s, pair):
    return [removed_s[pair * 16 + j] for j in range(16)]


def index_rows(indices, lanes):
    row = lax.broadcasted_iota(jnp.int32, (16, lanes), 0)
    out = jnp.full((16, lanes), -1, jnp.int32)
    for j, r in enumerate(indices):
        out = jnp.where(row == j, r, out)
    return out


def ranks(indices, first, lanes, rows=16):
    lane = lax.broadcasted_iota(jnp.int32, (rows, lanes), 1) + first
    shard = first
    below = jnp.zeros((rows, lanes), jnp.int32)
    gone = jnp.zeros((rows, lanes), jnp.int32)
    for r in indices:
        mine = jnp.where(r >= shard, 1, 0)
        below = below + jnp.where(r < lane, mine, 0)
        gone = gone + jnp.where(r == lane, 1, 0)
    return jnp.where(gone > 0, -1, lane - first - below)


def spread_kernel(
    removed_s, tok_ref, down_ref, damp_ref, removed_v, h_hbm,
    tok_o, l_o, s_o, hkr_o, slabd_o, slabh_o,
    hbuf, tokpad, lpad, spad, tok_rx, l_rx, s_rx, slabd_tx, slabh_tx,
    hsem, pair_s, pair_r, sc_s, sc_r, y_s, y_r, z_s, z_r, x_s, x_r, c_s, c_r, sl_s, sl_r,
):
    x, z, c, d = place()
    other = 1 - c
    pair = x * NZ + z
    first = (pair * 2 + c) * WIDTH
    quarter = FF // 4
    loads = [
        pltpu.make_async_copy(h_hbm.at[:, pl.ds(g * quarter, quarter)], hbuf.at[g], hsem.at[g]) for g in range(4)
    ]
    for load in loads:
        load.start()
    partner = at(x, z, other, d)
    right, left = at((x + 1) % NX, z, c, d), at((x + 3) % NX, z, c, d)
    ydev = [at(x, z, c, (d + k) % NY) for k in range(1, NY)]
    ycross = [at(x, z, other, (d + k) % NY) for k in range(1, NY)]
    zdev = [at(x, (z + k) % NZ, c, d) for k in range(1, NZ)]
    greet([partner, right, left] + ydev + ycross + zdev)

    indices = pair_indices(removed_s, pair)
    tok = tok_ref[...].astype(F32)
    none = jnp.zeros_like(tok)
    full = jnp.where(c == 0, jnp.concatenate([tok, none], axis=0), jnp.concatenate([none, tok], axis=0)).astype(BF)
    tokpad[0] = full[:, :1024]
    tokpad[1] = full[:, 1024:]
    tok_pair = remote(tokpad.at[other], tok_rx, pair_s.at[0], pair_r.at[0], partner)
    tok_pair.start()
    rows416 = index_rows(indices, WIDTH)
    lane416 = lax.broadcasted_iota(jnp.int32, (16, WIDTH), 1)
    pick = jnp.where(lane416 + first == rows416, 1.0, 0.0).astype(BF)
    lost = dot(pick, down_ref[...]).astype(BF)
    lpad[0] = lost[:, :1024]
    lpad[1] = lost[:, 1024:]
    l_pair = remote(lpad.at[other], l_rx, pair_s.at[1], pair_r.at[1], partner)
    l_pair.start()
    rank416 = ranks(indices, first, WIDTH)
    row16 = lax.broadcasted_iota(jnp.int32, (16, WIDTH), 0)
    target = jnp.where(row16 < 8, row16 + (1 - c) * KEPT, -7)
    slab_pick = jnp.where(rank416 == target, 1.0, 0.0)
    slabd_tx[...] = dot(slab_pick.astype(BF), down_ref[...]).astype(BF)
    slabd = remote(slabd_tx, slabd_o, sl_s.at[0], sl_r.at[0], partner)
    slabd.start()

    tok_pair.wait_recv()
    tok_o[c, x, z] = tokpad[c] + tok_rx[...]

    def z_sends(array, n):
        copies = [
            remote(array.at[c, x, z], array.at[c, x, z], z_s.at[n, k], z_r.at[n, k], zdev[k]) for k in range(NZ - 1)
        ]
        for copy in copies:
            copy.start()
        return copies

    tok_z = z_sends(tok_o, 0)
    l_pair.wait_recv()
    l_o[c, x, z] = lpad[c] + l_rx[...]
    l_z = z_sends(l_o, 1)

    chunk = quarter // 4
    for g in range(4):
        loads[g].wait()
        wanted = removed_v[:, g * 128 : (g + 1) * 128]
        total = jnp.zeros((BLOCK, 128), F32)
        for q in range(4):
            start = g * quarter + q * chunk
            channel = lax.broadcasted_iota(jnp.int32, (chunk, 128), 0) + start
            hot = jnp.where(channel == wanted, 1.0, 0.0).astype(BF)
            total = total + dot(hbuf[g, :, q * chunk : (q + 1) * chunk], hot)
        hkr_o[d, :, g * 128 : (g + 1) * 128] = total.astype(BF)
    rows104 = index_rows(indices, BLOCK)
    lane104 = lax.broadcasted_iota(jnp.int32, (16, BLOCK), 1)
    pick104 = jnp.where(lane104 + (first + d * BLOCK) == rows104, 1.0, 0.0)
    own_rows = dot(pick104.astype(BF), hkr_o[d]).astype(BF)
    damp = jnp.sum(pick104 * damp_ref[...], axis=1, keepdims=True)
    high = damp.astype(BF).astype(F32)
    lane128 = lax.broadcasted_iota(jnp.int32, (16, 128), 1)
    extra = jnp.where(lane128 == 0, high, jnp.where(lane128 == 1, damp - high, 0.0)).astype(BF)
    for half in range(2):
        spad[half, :, :256] = own_rows[:, half * 256 : (half + 1) * 256]
        spad[half, :, 256:] = extra
    s_sends = []
    for k in range(NY - 1):
        s_sends.append(remote(spad.at[c], s_rx.at[k], sc_s.at[k], sc_r.at[k], ydev[k]))
        s_sends.append(remote(spad.at[other], s_rx.at[3 + k], sc_s.at[3 + k], sc_r.at[3 + k], ycross[k]))
    s_sends.append(remote(spad.at[other], s_rx.at[6], sc_s.at[6], sc_r.at[6], partner))
    for copy in s_sends:
        copy.start()
    h_sends = [remote(hkr_o.at[d], hkr_o.at[d], y_s.at[k], y_r.at[k], ydev[k]) for k in range(NY - 1)]
    for copy in h_sends:
        copy.start()

    def x_sends(array, n):
        copies = [
            remote(array.at[c, x], array.at[c, x], x_s.at[n, 0], x_r.at[n, 0], right),
            remote(array.at[c, x], array.at[c, x], x_s.at[n, 1], x_r.at[n, 1], left),
        ]
        for copy in copies:
            copy.start()
        return copies

    def x_forwards(array, n):
        copies = [
            remote(
                array.at[c, (x + 3) % NX, pl.ds(0, 4)], array.at[c, (x + 3) % NX, pl.ds(0, 4)],
                x_s.at[n, 2], x_r.at[n, 2], right,
            ),
            remote(
                array.at[c, (x + 1) % NX, pl.ds(4, 4)], array.at[c, (x + 1) % NX, pl.ds(4, 4)],
                x_s.at[n, 3], x_r.at[n, 3], left,
            ),
        ]
        for copy in copies:
            copy.start()
        return copies

    def core_send(array, n, k):
        copy = remote(
            array.at[c, (x + k) % NX], array.at[c, (x + k) % NX], c_s.at[n, k], c_r.at[n, k], partner
        )
        copy.start()
        return copy

    started = []

    def stage_z(copies):
        for copy in copies:
            copy.wait_recv()

    stage_z(tok_z)
    tok_x = x_sends(tok_o, 0)
    tok_c = [core_send(tok_o, 0, 0)]
    for copy in s_sends:
        copy.wait_recv()
    total = spad[c].astype(F32)
    for k in range(7):
        total = total + s_rx[k].astype(F32)
    s_o[c, x, z] = total.astype(BF)
    s_z = z_sends(s_o, 2)
    stage_z(l_z)
    stage_z(s_z)
    s_x = x_sends(s_o, 2)
    s_c = [core_send(s_o, 2, 0)]
    stage_z(tok_x)
    tok_f = x_forwards(tok_o, 0)
    tok_c += [core_send(tok_o, 0, 1), core_send(tok_o, 0, 3)]
    l_x = x_sends(l_o, 1)
    l_c = [core_send(l_o, 1, 0)]
    stage_z(s_x)
    s_f = x_forwards(s_o, 2)
    s_c += [core_send(s_o, 2, 1), core_send(s_o, 2, 3)]
    stage_z(h_sends)
    slab = jnp.zeros((16, REM), F32)
    for k in range(NY):
        piece = jnp.where(ranks_piece(indices, first, k * BLOCK) == target[:, :BLOCK], 1.0, 0.0).astype(BF)
        slab = slab + dot(piece, hkr_o[k])
    slabh_tx[...] = slab.astype(BF)
    slabh = remote(slabh_tx, slabh_o, sl_s.at[1], sl_r.at[1], partner)
    slabh.start()
    stage_z(tok_f)
    tok_c.append(core_send(tok_o, 0, 2))
    stage_z(l_x)
    l_f = x_forwards(l_o, 1)
    l_c += [core_send(l_o, 1, 1), core_send(l_o, 1, 3)]
    stage_z(s_f)
    s_c.append(core_send(s_o, 2, 2))
    stage_z(l_f)
    l_c.append(core_send(l_o, 1, 2))
    stage_z(tok_c + s_c + l_c + [slabd, slabh])
    for copy in (
        [tok_pair, l_pair, slabd, slabh] + tok_z + l_z + s_z + s_sends + h_sends
        + tok_x + tok_f + tok_c + s_x + s_f + s_c + l_x + l_f + l_c
    ):
        copy.wait_send()


def ranks_piece(indices, first, offset):
    lane = lax.broadcasted_iota(jnp.int32, (16, BLOCK), 1) + (first + offset)
    below = jnp.zeros((16, BLOCK), jnp.int32)
    gone = jnp.zeros((16, BLOCK), jnp.int32)
    for r in indices:
        mine = jnp.where(r >= first, 1, 0)
        below = below + jnp.where(r < lane, mine, 0)
        gone = gone + jnp.where(r == lane, 1, 0)
    return jnp.where(gone > 0, -1, lane - first - below)


def hidden_kernel(removed_s, tok_ref, gate_ref, up_ref, hid_o, tx, rx, own, s_s, s_r, h_s, h_r):
    x, z, c, d = place()
    ydev = [at(x, z, c, (d + k) % NY) for k in range(1, NY)]
    greet(ydev)
    pair = x * NZ + z
    first = (pair * 2 + c) * WIDTH

    def partial(block, weight):
        total = dot(tok_ref[0, block], weight[:1024])
        return total + dot(tok_ref[1, block], weight[1024:])

    sends = []
    for k in range(1, NY):
        block = (d + k) % NY
        tx[k - 1, 0] = partial(block, gate_ref).astype(BF)
        tx[k - 1, 1] = partial(block, up_ref).astype(BF)
        copy = remote(tx.at[k - 1], rx.at[k - 1], s_s.at[k - 1], s_r.at[k - 1], ydev[k - 1])
        copy.start()
        sends.append(copy)
    own[0] = partial(d, gate_ref)
    own[1] = partial(d, up_ref)
    lane = lax.broadcasted_iota(jnp.int32, (8, WIDTH), 1) + first
    keep = jnp.ones((8, WIDTH), F32)
    for r in pair_indices(removed_s, pair):
        keep = jnp.where(lane == r, 0.0, keep)
    for copy in sends:
        copy.wait_recv()
    gate = own[0]
    up = own[1]
    for k in range(NY - 1):
        gate = gate + rx[k, 0].astype(F32)
        up = up + rx[k, 1].astype(F32)
    hidden = gate / (1.0 + jnp.exp(-gate)) * up
    hid_o[d] = jnp.where(keep[:1] > 0.0, hidden, 0.0).astype(BF)
    shares = [remote(hid_o.at[d], hid_o.at[d], h_s.at[k], h_r.at[k], ydev[k]) for k in range(NY - 1)]
    for copy in shares:
        copy.start()
    for copy in shares:
        copy.wait_recv()
    for copy in sends + shares:
        copy.wait_send()


def split(value):
    high = value.astype(BF)
    return high, (value - high.astype(F32)).astype(BF)


def compensate_kernel(
    removed_s, s_ref, l_ref, hkr_ref, slabh_ref, down_ref, slabd_ref, corr_o, pruned_o,
    sx, xy, xyh, xyl, rh, rl, rows, slabc, lanes,
):
    t = lax.axis_index("tensor")
    c = t % 2
    pair = t // 2
    eye = lax.broadcasted_iota(jnp.int32, (REM, REM), 0) == lax.broadcasted_iota(jnp.int32, (REM, REM), 1)
    damp = s_ref[0, :, 256:257].astype(F32) + s_ref[0, :, 257:258].astype(F32)
    sx[:, :256] = s_ref[0, :, :256].astype(F32)
    sx[:, 256:] = s_ref[1, :, :256].astype(F32)
    square = sx[...] + jnp.where(eye, damp, 0.0)
    bound = jnp.max(jnp.sum(jnp.abs(square), axis=0, keepdims=True), axis=1, keepdims=True)
    inverse_bound = 1.0 / bound
    low = 0.5 * inverse_bound
    xy[REM:, :] = square * inverse_bound
    xy[:REM, :] = jnp.where(eye, inverse_bound, 0.0)
    for step in range(STEPS):
        middle = 0.5 * (1.0 + low)
        gain = 1.0 / (middle * middle)
        factor = (jnp.where(eye, 2.0 * middle, 0.0) - xy[REM:, :]) * gain
        high, rest = split(factor)
        rh[...] = high
        rl[...] = rest
        parts = [0, 1] if step < STEPS - 1 else [0]
        for part in parts:
            if step == 0 and part == 0:
                xy[:REM, :] = factor * inverse_bound
                continue
            own = pl.ds(part * REM, REM)
            high, rest = split(xy[own, :])
            xyh[...] = high
            xyl[...] = rest
            xy[own, :] = dot(xyh[...], rh[...]) + (dot(xyh[...], rl[...]) + dot(xyl[...], rh[...]))
        low = low * gain
    high, rest = split(xy[:REM, :] * (2.0 / (1.0 + low)))
    rh[...] = high
    rl[...] = rest
    rows[:WIDTH] = hkr_ref[...]
    rows[WIDTH:] = slabh_ref[...]
    coef = dot(rows[...], rh[...]) + dot(rows[...], rl[...])
    high, rest = split(coef)
    for half in range(2):
        cols = pl.ds(half * 1024, 1024)
        change = dot(high, l_ref[half]) + dot(rest, l_ref[half])
        corr_o[:, cols] = (down_ref[:, cols].astype(F32) - change[:WIDTH]).astype(BF)
        slabc[:, cols] = (slabd_ref[:, cols].astype(F32) - change[WIDTH:]).astype(BF)
    indices = pair_indices(removed_s, pair)
    first = t * WIDTH
    even = (pair * 2 + 1) * WIDTH
    even_kept = WIDTH
    for r in indices:
        even_kept = even_kept - jnp.where(r < even, 1, 0)
    rank = ranks(indices, first, WIDTH, 8)
    goal = jnp.where(rank < 0, -1, rank + c * (even_kept - KEPT))[:1]
    row = lax.broadcasted_iota(jnp.int32, (KEPT, WIDTH), 0)
    pack = jnp.where(row == goal, 1.0, 0.0).astype(BF)
    lane = lax.broadcasted_iota(jnp.int32, (8, 16), 1)
    from_odd = even_kept + lane
    from_even = jnp.where(KEPT + lane < even_kept, lane, -1)
    slab_goal = jnp.where(lane < 8, jnp.where(c == 0, from_odd, from_even), -1)[:1]
    row = lax.broadcasted_iota(jnp.int32, (KEPT, 16), 0)
    slab_pack = jnp.where(row == slab_goal, 1.0, 0.0).astype(BF)
    for half in range(2):
        cols = pl.ds(half * 1024, 1024)
        pruned_o[:, cols] = (dot(pack, corr_o[:, cols]) + dot(slab_pack, slabc[:, cols])).astype(BF)


def mixed_kernel(
    hid_ref, corr_ref, out_ref,
    ptx, prx, own, x2, xa, xb, xtx, xrx, ztx, zrx, fin, frx,
    p_s, p_r, a_s, a_r, x_s, x_r, z_s, z_r, f_s, f_r,
):
    x, z, c, d = place()
    other = 1 - c
    partner = at(x, z, other, d)
    right, left = at((x + 1) % NX, z, c, d), at((x + 3) % NX, z, c, d)
    zdev = [at(x, (z + k) % NZ, c, d) for k in range(1, NZ)]
    greet([partner, right, left] + zdev)
    scale = FF ** (-0.5)
    order = (2, 1, 3, 0)
    mine = pl.ds(pl.multiple_of(c * 1024, 1024), 1024)
    theirs = pl.ds(pl.multiple_of(other * 1024, 1024), 1024)
    pairs = {}
    for k in order:
        ptx[k] = (dot(hid_ref[(x + k) % NX], corr_ref[:, theirs]) * scale).astype(BF)
        pairs[k] = remote(ptx.at[k], prx.at[k], p_s.at[k], p_r.at[k], partner)
        pairs[k].start()
    for k in order:
        own[k] = dot(hid_ref[(x + k) % NX], corr_ref[:, mine]) * scale
    pairs[2].wait_recv()
    x2[...] = (own[2] + prx[2].astype(F32)).astype(BF)
    to_right = remote(x2.at[pl.ds(0, 64)], xa, a_s.at[0], a_r.at[0], right)
    to_left = remote(x2.at[pl.ds(64, 64)], xb, a_s.at[1], a_r.at[1], left)
    to_right.start()
    to_left.start()
    pairs[1].wait_recv()
    own[1] = own[1] + prx[1].astype(F32)
    pairs[3].wait_recv()
    own[3] = own[3] + prx[3].astype(F32)
    xtx[0, 64:] = own[1, 64:].astype(BF)
    xtx[1, :64] = own[3, :64].astype(BF)
    low, high = pl.ds(0, 64), pl.ds(64, 64)
    plain = [
        remote(xtx.at[0, high], xrx.at[0, high], x_s.at[0], x_r.at[0], right),
        remote(xtx.at[1, low], xrx.at[1, low], x_s.at[1], x_r.at[1], left),
    ]
    for copy in plain:
        copy.start()
    to_right.wait_recv()
    xtx[0, :64] = (own[1, :64] + xa[...].astype(F32)).astype(BF)
    to_left.wait_recv()
    xtx[1, 64:] = (own[3, 64:] + xb[...].astype(F32)).astype(BF)
    summed = [
        remote(xtx.at[0, low], xrx.at[0, low], x_s.at[2], x_r.at[2], right),
        remote(xtx.at[1, high], xrx.at[1, high], x_s.at[3], x_r.at[3], left),
    ]
    for copy in summed:
        copy.start()
    pairs[0].wait_recv()
    total = own[0] + prx[0].astype(F32)
    for copy in plain + summed:
        copy.wait_recv()
    own[0] = total + xrx[0].astype(F32) + xrx[1].astype(F32)
    zs = []
    for k in range(1, NZ):
        rows = pl.ds(pl.multiple_of(((z + k) % NZ) * 16, 16), 16)
        ztx[k - 1] = own[0, rows].astype(BF)
        copy = remote(ztx.at[k - 1], zrx.at[k - 1], z_s.at[k - 1], z_r.at[k - 1], zdev[k - 1])
        copy.start()
        zs.append(copy)
    total = own[0, pl.ds(pl.multiple_of(z * 16, 16), 16)]
    for k in range(NZ - 1):
        zs[k].wait_recv()
        total = total + zrx[k].astype(F32)
    fin[0] = total[:8]
    fin[1] = total[8:]
    last = remote(fin.at[other], frx, f_s.at[0], f_r.at[0], partner)
    last.start()
    out_ref[:, mine] = fin[c].astype(BF)
    last.wait_recv()
    out_ref[:, theirs] = frx[...].astype(BF)
    for copy in list(pairs.values()) + [to_right, to_left] + plain + summed + zs + [last]:
        copy.wait_send()


def dma(*shape):
    return pltpu.SemaphoreType.DMA(shape)


def vmem():
    return pl.BlockSpec(memory_space=pltpu.VMEM)


def smem():
    return pl.BlockSpec(memory_space=pltpu.SMEM)


def params(collective):
    return pltpu.CompilerParams(
        collective_id=collective, has_side_effects=True, vmem_limit_bytes=VMEM_LIMIT
    )


def out(*shape):
    return jax.ShapeDtypeStruct(shape, BF)


def shards(tokens, gate_weight, up_weight, down_weight, inverse_hessian, damping, removed):
    t = lax.axis_index("tensor")
    d = lax.axis_index("dp")
    own_damp = lax.dynamic_slice(damping, (t * WIDTH + d * BLOCK,), (BLOCK,)).reshape(1, BLOCK)
    tok_all, l_all, s_all, hkr, slab_down, slab_h = pl.pallas_call(
        spread_kernel,
        out_shape=(
            out(2, NX, NZ, 16, 1024), out(2, NX, NZ, 16, 1024), out(2, NX, NZ, 16, 384),
            out(NY, BLOCK, REM), out(16, 2048), out(16, REM),
        ),
        in_specs=[smem(), vmem(), vmem(), vmem(), vmem(), pl.BlockSpec(memory_space=pl.ANY)],
        out_specs=tuple(vmem() for _ in range(6)),
        scratch_shapes=[
            pltpu.VMEM((4, BLOCK, FF // 4), BF),
            pltpu.VMEM((2, 16, 1024), BF), pltpu.VMEM((2, 16, 1024), BF), pltpu.VMEM((2, 16, 384), BF),
            pltpu.VMEM((16, 1024), BF), pltpu.VMEM((16, 1024), BF), pltpu.VMEM((7, 16, 384), BF),
            pltpu.VMEM((16, 2048), BF), pltpu.VMEM((16, REM), BF),
            dma(4), dma(2), dma(2), dma(7), dma(7), dma(3), dma(3), dma(3, 7), dma(3, 7),
            dma(3, 4), dma(3, 4), dma(3, 4), dma(3, 4), dma(2), dma(2),
        ],
        compiler_params=params(1),
        name="spread",
    )(removed, tokens, down_weight, own_damp, removed.reshape(1, REM), inverse_hessian)
    hidden = pl.pallas_call(
        hidden_kernel,
        out_shape=out(NY, 128, WIDTH),
        in_specs=[smem(), vmem(), vmem(), vmem()],
        out_specs=vmem(),
        scratch_shapes=[
            pltpu.VMEM((3, 2, 128, WIDTH), BF), pltpu.VMEM((3, 2, 128, WIDTH), BF),
            pltpu.VMEM((2, 128, WIDTH), F32), dma(3), dma(3), dma(3), dma(3),
        ],
        compiler_params=params(2),
        name="hidden",
    )(removed, tok_all.reshape(2, NY, 128, 1024), gate_weight, up_weight)
    corrected, pruned = pl.pallas_call(
        compensate_kernel,
        out_shape=(out(WIDTH, 2048), out(KEPT, 2048)),
        in_specs=[smem()] + [vmem()] * 6,
        out_specs=(vmem(), vmem()),
        scratch_shapes=[
            pltpu.VMEM((REM, REM), F32), pltpu.VMEM((2 * REM, REM), F32),
            pltpu.VMEM((REM, REM), BF), pltpu.VMEM((REM, REM), BF),
            pltpu.VMEM((REM, REM), BF), pltpu.VMEM((REM, REM), BF),
            pltpu.VMEM((WIDTH + 16, REM), BF), pltpu.VMEM((16, 2048), BF), pltpu.VMEM((8, 128), F32),
        ],
        compiler_params=pltpu.CompilerParams(vmem_limit_bytes=VMEM_LIMIT),
        name="compensate",
    )(
        removed, s_all.reshape(2, REM, 384), l_all.reshape(2, REM, 1024), hkr.reshape(WIDTH, REM), slab_h,
        down_weight, slab_down,
    )
    mixed = pl.pallas_call(
        mixed_kernel,
        out_shape=out(8, 2048),
        in_specs=[vmem(), vmem()],
        out_specs=vmem(),
        scratch_shapes=[
            pltpu.VMEM((4, 128, 1024), BF), pltpu.VMEM((4, 128, 1024), BF), pltpu.VMEM((4, 128, 1024), F32),
            pltpu.VMEM((128, 1024), BF), pltpu.VMEM((64, 1024), BF), pltpu.VMEM((64, 1024), BF),
            pltpu.VMEM((2, 128, 1024), BF), pltpu.VMEM((2, 128, 1024), BF),
            pltpu.VMEM((7, 16, 1024), BF), pltpu.VMEM((7, 16, 1024), BF),
            pltpu.VMEM((2, 8, 1024), F32), pltpu.VMEM((8, 1024), F32),
            dma(4), dma(4), dma(2), dma(2), dma(4), dma(4), dma(7), dma(7), dma(1), dma(1),
        ],
        compiler_params=params(3),
        name="mixed",
    )(hidden, corrected)
    return pruned, mixed


def solution(mesh):
    in_specs = (
        P("tensor", "dp"),
        P("dp", "tensor"),
        P("dp", "tensor"),
        P("tensor", "dp"),
        P(("tensor", "dp"), None),
        P(),
        P(),
    )
    out_specs = (P("tensor", "dp"), P("tensor", "dp"))
    return jax.shard_map(shards, mesh=mesh, in_specs=in_specs, out_specs=out_specs, check_vma=False)
```

```python
import jax
import jax.numpy as jnp
from jax import lax
from jax.experimental import pallas as pl
from jax.experimental.pallas import tpu as pltpu
from jax.sharding import PartitionSpec as P

MESH = pl.DeviceIdType.MESH
BF = jnp.bfloat16
F32 = jnp.float32
NX, NZ, NY = 4, 8, 4
WIDTH = 416
BLOCK = 104
KEPT = 408
FF = 26624
REM = 512
STEPS = 8
HALF = REM // 2
VMEM_LIMIT = 56 * 1024 * 1024


def dot(a, b):
    return jnp.dot(a, b, preferred_element_type=F32)


def place():
    t = lax.axis_index("tensor")
    d = lax.axis_index("dp")
    return t // 16, (t // 2) % 8, t % 2, d


def at(x, z, c, d):
    return (x * 16 + z * 2 + c, d)


def remote(src, dst, send, recv, device):
    return pltpu.make_async_remote_copy(
        src_ref=src, dst_ref=dst, send_sem=send, recv_sem=recv, device_id=device, device_id_type=MESH
    )


def greet(devices):
    barrier = pltpu.get_barrier_semaphore()
    for device in devices:
        pl.semaphore_signal(barrier, inc=1, device_id=device, device_id_type=MESH)
    pl.semaphore_wait(barrier, len(devices))


def pair_indices(removed_s, pair):
    return [removed_s[pair * 16 + j] for j in range(16)]


def index_rows(indices, lanes):
    row = lax.broadcasted_iota(jnp.int32, (16, lanes), 0)
    out = jnp.full((16, lanes), -1, jnp.int32)
    for j, r in enumerate(indices):
        out = jnp.where(row == j, r, out)
    return out


def dot_nt(a, b):
    return lax.dot_general(a, b, (((1,), (1,)), ((), ())), preferred_element_type=F32)


def ranks(indices, first, offset, lanes, rows=16):
    lane = lax.broadcasted_iota(jnp.int32, (rows, lanes), 1) + (first + offset)
    below = jnp.zeros((rows, lanes), jnp.int32)
    gone = jnp.zeros((rows, lanes), jnp.int32)
    for r in indices:
        mine = jnp.where(r >= first, 1, 0)
        below = below + jnp.where(r < lane, mine, 0)
        gone = gone + jnp.where(r == lane, 1, 0)
    return jnp.where(gone > 0, -1, lane - first - below)


def split(value):
    high = value.astype(BF)
    return high, (value - high.astype(F32)).astype(BF)


def dot2(pair, b):
    return dot(pair[0], b) + dot(pair[1], b)


def dot3(a, b):
    return dot(a[0], b[0]) + (dot(a[0], b[1]) + dot(a[1], b[0]))


def newton(xy, between):
    n = HALF
    eye = lax.broadcasted_iota(jnp.int32, (n, n), 0) == lax.broadcasted_iota(jnp.int32, (n, n), 1)
    square = xy[n:, :]
    bound = jnp.max(jnp.sum(jnp.abs(square), axis=0, keepdims=True), axis=1, keepdims=True)
    inverse_bound = 1.0 / bound
    low = 0.5 * inverse_bound
    xy[n:, :] = square * inverse_bound
    for step in range(STEPS):
        middle = 0.5 * (1.0 + low)
        gain = 1.0 / (middle * middle)
        factor = (jnp.where(eye, 2.0 * middle, 0.0) - xy[n:, :]) * gain
        right = split(factor)
        if step == 0:
            xy[n:, :] = dot3(split(xy[n:, :]), right)
            xy[:n, :] = factor * inverse_bound
        elif step < STEPS - 1:
            xy[...] = dot3(split(xy[...]), right)
        else:
            xy[:n, :] = dot3(split(xy[:n, :]), right)
        low = low * gain
        between(step)
    xy[:n, :] = xy[:n, :] * (2.0 / (1.0 + low))


def prune_kernel(
    removed_s, tok_h, gate_h, up_h, down_h, hess_h, damp_h, removed_h,
    pruned_o, mixed_o,
    tok_in, down, damp, removed_v, hbuf, weight,
    tok_o, l_o, s_o, hkr_o, slabd_o, slabh_o,
    lpad, spad, l_rx, s_rx, slabd_tx, slabh_tx,
    lhs, pre, pre_tx, pre_rx, pre_own, hid,
    xy, inv, rows, corr, slabc,
    ptx, prx, own, x2, xa, xb, xtx, xrx, ztx, zrx, fin, frx,
    load_s, hess_s, pair_s, pair_r, sc_s, sc_r, y_s, y_r, z_s, z_r, x_s, x_r, c_s, c_r, sl_s, sl_r,
    ps_s, ps_r, h_s, h_r,
    p_s, p_r, a_s, a_r, e_s, e_r, w_s, w_r, f_s, f_r,
):
    x, z, c, d = place()
    other = 1 - c
    pair = x * NZ + z
    first = (pair * 2 + c) * WIDTH
    quarter = FF // 4

    def load(src, dst, sem):
        copy = pltpu.make_async_copy(src, dst, sem)
        copy.start()
        return copy

    tok_load = load(tok_h, tok_in, load_s.at[0])
    removed_load = load(removed_h, removed_v, load_s.at[1])
    damp_load = load(damp_h, damp, load_s.at[2])
    hess_loads = [load(hess_h.at[:, pl.ds(g * quarter, quarter)], hbuf.at[g], hess_s.at[g]) for g in range(4)]
    down_load = load(down_h, down, load_s.at[3])
    gate_load = load(gate_h, weight.at[pl.ds(0, WIDTH)], load_s.at[4])
    up_load = load(up_h, weight.at[pl.ds(WIDTH, WIDTH)], load_s.at[5])

    partner = at(x, z, other, d)
    right, left = at((x + 1) % NX, z, c, d), at((x + 3) % NX, z, c, d)
    ydev = [at(x, z, c, (d + k) % NY) for k in range(1, NY)]
    ycross = [at(x, z, other, (d + k) % NY) for k in range(1, NY)]
    zdev = [at(x, (z + k) % NZ, c, d) for k in range(1, NZ)]
    greet([partner, right, left] + ydev + ycross + zdev)
    pending = []

    def send(src, dst, s, r, device):
        copy = remote(src, dst, s, r, device)
        copy.start()
        pending.append(copy)
        return copy

    def arrived(copies):
        for copy in copies:
            copy.wait_recv()

    def z_sends(array, n):
        here = array.at[c, x, z]
        return [send(here, here, z_s.at[n, k], z_r.at[n, k], zdev[k]) for k in range(NZ - 1)]

    def x_sends(array, n):
        here = array.at[c, x]
        return [
            send(here, here, x_s.at[n, 0], x_r.at[n, 0], right),
            send(here, here, x_s.at[n, 1], x_r.at[n, 1], left),
        ]

    def x_forwards(array, n):
        low = array.at[c, (x + 3) % NX, pl.ds(0, 4)]
        high = array.at[c, (x + 1) % NX, pl.ds(4, 4)]
        return [
            send(low, low, x_s.at[n, 2], x_r.at[n, 2], right),
            send(high, high, x_s.at[n, 3], x_r.at[n, 3], left),
        ]

    def core_send(array, n, k):
        here = array.at[c, (x + k) % NX]
        return send(here, here, c_s.at[n, k], c_r.at[n, k], partner)

    tok_load.wait()
    tok = tok_in[...].astype(F32)
    tok_o[c, x, z] = jnp.concatenate([tok[:, :1024], tok[:, 1024:]], axis=0).astype(BF)
    tok_z = z_sends(tok_o, 0)

    indices = pair_indices(removed_s, pair)
    removed_load.wait()
    chunk = quarter // 4
    for g in range(4):
        hess_loads[g].wait()
        wanted = removed_v[g : g + 1, :]
        total = jnp.zeros((BLOCK, 128), F32)
        for q in range(4):
            start = g * quarter + q * chunk
            channel = lax.broadcasted_iota(jnp.int32, (chunk, 128), 0) + start
            hot = jnp.where(channel == wanted, 1.0, 0.0).astype(BF)
            total = total + dot(hbuf[g, :, q * chunk : (q + 1) * chunk], hot)
        hkr_o[d, :, g * 128 : (g + 1) * 128] = total.astype(BF)
    rows104 = index_rows(indices, BLOCK)
    lane104 = lax.broadcasted_iota(jnp.int32, (16, BLOCK), 1)
    block_first = first + d * BLOCK
    pick104 = jnp.where(lane104 + block_first == rows104, 1.0, 0.0)
    own_rows = dot(pick104.astype(BF), hkr_o[d]).astype(BF)
    damp_load.wait()
    lane128 = lax.broadcasted_iota(jnp.int32, (16, 128), 1)
    row128 = lax.broadcasted_iota(jnp.int32, (16, 128), 0)
    found = jnp.zeros((16, 128), F32)
    for j, r in enumerate(indices):
        line = damp[pl.ds(r // 128, 1), :]
        here = jnp.where(r >= block_first, jnp.where(r < block_first + BLOCK, j, -1), -1)
        found = jnp.where(row128 == here, jnp.where(lane128 == r % 128, line, 0.0), found)
    damped = jnp.sum(found, axis=1, keepdims=True)
    high = damped.astype(BF).astype(F32)
    extra = jnp.where(lane128 == 0, high, jnp.where(lane128 == 1, damped - high, 0.0)).astype(BF)
    for half in range(2):
        spad[half, :, :256] = own_rows[:, half * 256 : (half + 1) * 256]
        spad[half, :, 256:] = extra
    s_sends = []
    for k in range(NY - 1):
        s_sends.append(send(spad.at[c], s_rx.at[k], sc_s.at[k], sc_r.at[k], ydev[k]))
        s_sends.append(send(spad.at[other], s_rx.at[3 + k], sc_s.at[3 + k], sc_r.at[3 + k], ycross[k]))
    s_sends.append(send(spad.at[other], s_rx.at[6], sc_s.at[6], sc_r.at[6], partner))
    h_sends = [send(hkr_o.at[d], hkr_o.at[d], y_s.at[k], y_r.at[k], ydev[k]) for k in range(NY - 1)]

    down_load.wait()
    rows416 = index_rows(indices, WIDTH)
    lane416 = lax.broadcasted_iota(jnp.int32, (16, WIDTH), 1)
    pick = jnp.where(lane416 + first == rows416, 1.0, 0.0).astype(BF)
    lost = dot(pick, down[...]).astype(BF)
    lpad[0] = lost[:, :1024]
    lpad[1] = lost[:, 1024:]
    l_pair = send(lpad.at[other], l_rx, pair_s.at[0], pair_r.at[0], partner)
    row16 = lax.broadcasted_iota(jnp.int32, (16, WIDTH), 0)
    target = jnp.where(row16 < 8, row16 + (1 - c) * KEPT, -7)
    slab_pick = jnp.where(ranks(indices, first, 0, WIDTH) == target, 1.0, 0.0)
    slabd_tx[...] = dot(slab_pick.astype(BF), down[...]).astype(BF)
    slabd = send(slabd_tx, slabd_o, sl_s.at[0], sl_r.at[0], partner)

    arrived(tok_z)
    tok_x = x_sends(tok_o, 0)
    tok_c = {0: core_send(tok_o, 0, 0)}
    arrived(s_sends)
    total = spad[c].astype(F32)
    for k in range(7):
        total = total + s_rx[k].astype(F32)
    s_o[c, x, z] = total.astype(BF)
    s_z = z_sends(s_o, 2)

    partials = {}

    def preact(k):
        arrived([tok_c[k]])
        b = (x + k) % NX
        for core in range(2):
            value = tok_o[core, b].astype(F32)
            lhs[0, core * 64 : core * 64 + 64] = value[:, :8].reshape(64, 1024).astype(BF)
            lhs[1, core * 64 : core * 64 + 64] = value[:, 8:].reshape(64, 1024).astype(BF)
        pre[...] = dot_nt(lhs[0], weight[:, :1024]) + dot_nt(lhs[1], weight[:, 1024:])
        sends = []
        for m in range(NY - 1):
            part = pl.ds(pl.multiple_of(((d + 1 + m) % NY) * 32, 32), 32)
            pre_tx[k, m] = pre[part, :].astype(BF)
            sends.append(send(pre_tx.at[k, m], pre_rx.at[k, m], ps_s.at[k, m], ps_r.at[k, m], ydev[m]))
        pre_own[k] = pre[pl.ds(pl.multiple_of(d * 32, 32), 32), :]
        partials[k] = sends

    shares = {}

    def gated(k):
        arrived(partials[k])
        value = pre_own[k]
        for m in range(NY - 1):
            value = value + pre_rx[k, m].astype(F32)
        gate, up = value[:, :WIDTH], value[:, WIDTH:]
        lane = lax.broadcasted_iota(jnp.int32, (32, WIDTH), 1) + first
        hidden = gate / (1.0 + jnp.exp(-gate)) * up
        for r in indices:
            hidden = jnp.where(lane == r, 0.0, hidden)
        hid[k, d] = hidden.astype(BF)
        here = hid.at[k, d]
        shares[k] = [send(here, here, h_s.at[k, m], h_r.at[k, m], ydev[m]) for m in range(NY - 1)]

    gate_load.wait()
    up_load.wait()
    preact(0)
    arrived(s_z)
    s_x = x_sends(s_o, 2)
    s_c = [core_send(s_o, 2, 0)]
    arrived(tok_x)
    tok_f = x_forwards(tok_o, 0)
    tok_c[1] = core_send(tok_o, 0, 1)
    tok_c[3] = core_send(tok_o, 0, 3)
    arrived(s_x)
    s_f = x_forwards(s_o, 2)
    s_c += [core_send(s_o, 2, 1), core_send(s_o, 2, 3)]
    preact(1)
    preact(3)
    arrived(s_f)
    s_c.append(core_send(s_o, 2, 2))
    arrived([l_pair])
    l_o[c, x, z] = lpad[c] + l_rx[...]
    l_z = z_sends(l_o, 1)
    arrived(tok_f)
    tok_c[2] = core_send(tok_o, 0, 2)
    arrived(s_c)

    later = {}

    def lost_x():
        arrived(l_z)
        later["x"] = x_sends(l_o, 1)
        later["c"] = [core_send(l_o, 1, 0)]

    def lost_forward():
        arrived(later["x"])
        later["f"] = x_forwards(l_o, 1)
        later["c"] += [core_send(l_o, 1, 1), core_send(l_o, 1, 3)]

    def lost_last():
        arrived(later["f"])
        later["c"].append(core_send(l_o, 1, 2))

    def gather_rows():
        arrived(h_sends)
        slab = jnp.zeros((16, REM), F32)
        for k in range(NY):
            mine = ranks(indices, first, k * BLOCK, BLOCK) == target[:, :BLOCK]
            slab = slab + dot(jnp.where(mine, 1.0, 0.0).astype(BF), hkr_o[k])
            rows[k * BLOCK : (k + 1) * BLOCK] = hkr_o[k].astype(F32)
        slabh_tx[...] = slab.astype(BF)
        later["s"] = send(slabh_tx, slabh_o, sl_s.at[1], sl_r.at[1], partner)

    eye = lax.broadcasted_iota(jnp.int32, (HALF, HALF), 0) == lax.broadcasted_iota(jnp.int32, (HALF, HALF), 1)

    def s_block(i, j):
        return s_o[j, 2 * i : 2 * i + 2, :, :, :256].reshape(HALF, 256)

    def diagonal(i):
        damping = s_o[0, 2 * i : 2 * i + 2, :, :, 256:].reshape(HALF, 128).astype(F32)
        return jnp.where(eye, damping[:, 0:1] + damping[:, 1:2], 0.0)

    xy[HALF:, :] = s_block(0, 0).astype(F32) + diagonal(0)
    tasks = {
        0: [lambda: preact(2)], 1: [lost_x], 2: [lambda: gated(0)], 4: [lambda: gated(1), lambda: gated(3)],
        5: [lost_forward], 7: [lambda: gated(2), gather_rows],
    }

    def first_tasks(step):
        for task in tasks.get(step, []):
            task()

    newton(xy, first_tasks)
    inv[...] = xy[:HALF, :]
    a_inv = split(inv[...])
    b_block = s_block(0, 1)
    v = dot(s_block(1, 0), a_inv[0]) + dot(s_block(1, 0), a_inv[1])
    xy[HALF:, :] = s_block(1, 1).astype(F32) + diagonal(1) - dot2(split(v), b_block)
    newton(xy, lambda step: lost_last() if step == 1 else None)
    e_inv = split(xy[:HALF, :])
    arrived([slabd, later["s"]])
    rows[WIDTH:] = slabh_o[...].astype(F32)
    q = dot(rows[:, :HALF].astype(BF), a_inv[0]) + dot(rows[:, :HALF].astype(BF), a_inv[1])
    u = rows[:, HALF:] - dot2(split(q), b_block)
    second = dot3(split(u), e_inv)
    pair_first = split(q - dot3(split(second), split(v)))
    pair_second = split(second)
    arrived(later["c"])
    lost_all = [l_o[h].reshape(REM, 1024) for h in range(2)]
    for half in range(2):
        cols = pl.ds(half * 1024, 1024)
        change = dot2(pair_first, lost_all[half][:HALF]) + dot2(pair_second, lost_all[half][HALF:])
        corr[:, cols] = (down[:, cols].astype(F32) - change[:WIDTH]).astype(BF)
        slabc[:, cols] = (slabd_o[:, cols].astype(F32) - change[WIDTH:]).astype(BF)

    scale = FF ** (-0.5)
    order = (2, 1, 3, 0)
    mine = pl.ds(pl.multiple_of(c * 1024, 1024), 1024)
    theirs = pl.ds(pl.multiple_of(other * 1024, 1024), 1024)
    pairs = {}
    for k in order:
        arrived(shares[k])
        ptx[k] = (dot(hid[k].reshape(128, WIDTH), corr[:, theirs]) * scale).astype(BF)
        pairs[k] = send(ptx.at[k], prx.at[k], p_s.at[k], p_r.at[k], partner)
    for k in order:
        own[k] = dot(hid[k].reshape(128, WIDTH), corr[:, mine]) * scale
    arrived([pairs[2]])
    x2[...] = (own[2] + prx[2].astype(F32)).astype(BF)
    low, top = pl.ds(0, 64), pl.ds(64, 64)
    to_right = send(x2.at[low], xa, a_s.at[0], a_r.at[0], right)
    to_left = send(x2.at[top], xb, a_s.at[1], a_r.at[1], left)
    arrived([pairs[1]])
    own[1] = own[1] + prx[1].astype(F32)
    xtx[0, 64:] = own[1, 64:].astype(BF)
    plain = [send(xtx.at[0, top], xrx.at[0, top], e_s.at[0], e_r.at[0], right)]
    arrived([pairs[3]])
    own[3] = own[3] + prx[3].astype(F32)
    xtx[1, :64] = own[3, :64].astype(BF)
    plain.append(send(xtx.at[1, low], xrx.at[1, low], e_s.at[1], e_r.at[1], left))

    even = (pair * 2 + 1) * WIDTH
    even_kept = WIDTH
    for r in indices:
        even_kept = even_kept - jnp.where(r < even, 1, 0)
    rank = ranks(indices, first, 0, WIDTH, 8)
    goal = jnp.where(rank < 0, -1, rank + c * (even_kept - KEPT))[:1]
    row = lax.broadcasted_iota(jnp.int32, (KEPT, WIDTH), 0)
    pack = jnp.where(row == goal, 1.0, 0.0).astype(BF)
    lane = lax.broadcasted_iota(jnp.int32, (8, 16), 1)
    from_odd = even_kept + lane
    from_even = jnp.where(KEPT + lane < even_kept, lane, -1)
    slab_goal = jnp.where(lane < 8, jnp.where(c == 0, from_odd, from_even), -1)[:1]
    row = lax.broadcasted_iota(jnp.int32, (KEPT, 16), 0)
    slab_pack = jnp.where(row == slab_goal, 1.0, 0.0).astype(BF)

    def packed(half):
        cols = pl.ds(half * 1024, 1024)
        pruned_o[:, cols] = (dot(pack, corr[:, cols]) + dot(slab_pack, slabc[:, cols])).astype(BF)

    packed(0)
    arrived([to_right])
    xtx[0, :64] = (own[1, :64] + xa[...].astype(F32)).astype(BF)
    summed = [send(xtx.at[0, low], xrx.at[0, low], e_s.at[2], e_r.at[2], right)]
    arrived([to_left])
    xtx[1, 64:] = (own[3, 64:] + xb[...].astype(F32)).astype(BF)
    summed.append(send(xtx.at[1, top], xrx.at[1, top], e_s.at[3], e_r.at[3], left))
    packed(1)
    arrived([pairs[0]])
    total = own[0] + prx[0].astype(F32)
    arrived(plain + summed)
    own[0] = total + xrx[0].astype(F32) + xrx[1].astype(F32)

    def z_rows(k):
        start = pl.multiple_of(((z + k) % NZ) * 8, 8)
        return jnp.concatenate([own[0, pl.ds(start, 8)], own[0, pl.ds(64 + start, 8)]], axis=0)

    zs = []
    for k in range(1, NZ):
        ztx[k - 1] = z_rows(k).astype(BF)
        zs.append(send(ztx.at[k - 1], zrx.at[k - 1], w_s.at[k - 1], w_r.at[k - 1], zdev[k - 1]))
    total = z_rows(0)
    for k in range(NZ - 1):
        arrived([zs[k]])
        total = total + zrx[k].astype(F32)
    fin[0] = total[:8]
    fin[1] = total[8:]
    last = send(fin.at[other], frx, f_s.at[0], f_r.at[0], partner)
    mixed_o[:, mine] = fin[c].astype(BF)
    arrived([last])
    mixed_o[:, theirs] = frx[...].astype(BF)
    for copy in pending:
        copy.wait_send()


def dma(*shape):
    return pltpu.SemaphoreType.DMA(shape)


def vmem():
    return pl.BlockSpec(memory_space=pltpu.VMEM)


def hbm():
    return pl.BlockSpec(memory_space=pl.ANY)


def out(*shape):
    return jax.ShapeDtypeStruct(shape, BF)


def shards(tokens, gate_weight, up_weight, down_weight, inverse_hessian, damping, removed):
    def bf(*shape):
        return pltpu.VMEM(shape, BF)

    def f32(*shape):
        return pltpu.VMEM(shape, F32)

    return pl.pallas_call(
        prune_kernel,
        out_shape=(out(KEPT, 2048), out(8, 2048)),
        in_specs=[pl.BlockSpec(memory_space=pltpu.SMEM)] + [hbm()] * 7,
        out_specs=(vmem(), vmem()),
        scratch_shapes=[
            bf(8, 2048), bf(WIDTH, 2048), f32(FF // 128, 128), pltpu.VMEM((4, 128), jnp.int32),
            bf(4, BLOCK, FF // 4), bf(2 * WIDTH, 2048),
            bf(2, NX, NZ, 16, 1024), bf(2, NX, NZ, 16, 1024), bf(2, NX, NZ, 16, 384),
            bf(NY, BLOCK, REM), bf(16, 2048), bf(16, REM),
            bf(2, 16, 1024), bf(2, 16, 384), bf(16, 1024), bf(7, 16, 384), bf(16, 2048), bf(16, REM),
            bf(2, 128, 1024), f32(128, 2 * WIDTH), bf(4, 3, 32, 2 * WIDTH), bf(4, 3, 32, 2 * WIDTH),
            f32(4, 32, 2 * WIDTH), bf(4, NY, 32, WIDTH),
            f32(2 * HALF, HALF), f32(HALF, HALF), f32(WIDTH + 16, REM), bf(WIDTH, 2048), bf(16, 2048),
            bf(4, 128, 1024), bf(4, 128, 1024), f32(4, 128, 1024), bf(128, 1024), bf(64, 1024), bf(64, 1024),
            bf(2, 128, 1024), bf(2, 128, 1024), bf(7, 16, 1024), bf(7, 16, 1024), f32(2, 8, 1024), f32(8, 1024),
            dma(6), dma(4), dma(1), dma(1), dma(7), dma(7), dma(3), dma(3), dma(3, 7), dma(3, 7),
            dma(3, 4), dma(3, 4), dma(3, 4), dma(3, 4), dma(2), dma(2),
            dma(4, 3), dma(4, 3), dma(4, 3), dma(4, 3),
            dma(4), dma(4), dma(2), dma(2), dma(4), dma(4), dma(7), dma(7), dma(1), dma(1),
        ],
        compiler_params=pltpu.CompilerParams(
            collective_id=1, has_side_effects=True, vmem_limit_bytes=VMEM_LIMIT
        ),
        name="prune",
    )(
        removed, tokens, gate_weight.T, up_weight.T, down_weight, inverse_hessian,
        damping.reshape(FF // 128, 128), removed.reshape(4, 128),
    )


def solution(mesh):
    in_specs = (
        P("tensor", "dp"),
        P("dp", "tensor"),
        P("dp", "tensor"),
        P("tensor", "dp"),
        P(("tensor", "dp"), None),
        P(),
        P(),
    )
    out_specs = (P("tensor", "dp"), P("tensor", "dp"))
    return jax.shard_map(shards, mesh=mesh, in_specs=in_specs, out_specs=out_specs, check_vma=False)
```

```python
import jax
import jax.numpy as jnp
from jax import lax
from jax.experimental import pallas as pl
from jax.experimental.pallas import tpu as pltpu
from jax.sharding import PartitionSpec as P

MESH = pl.DeviceIdType.MESH
BF = jnp.bfloat16
F32 = jnp.float32
NX, NZ, NY = 4, 8, 4
WIDTH = 416
BLOCK = 104
KEPT = 408
FF = 26624
REM = 512
STEPS = 8
HALF = REM // 2
PIECES = 8
VMEM_LIMIT = 56 * 1024 * 1024


def dot(a, b):
    return jnp.dot(a, b, preferred_element_type=F32)


def place():
    t = lax.axis_index("tensor")
    d = lax.axis_index("dp")
    return t // 16, (t // 2) % 8, t % 2, d


def at(x, z, c, d):
    return (x * 16 + z * 2 + c, d)


def remote(src, dst, send, recv, device):
    return pltpu.make_async_remote_copy(
        src_ref=src, dst_ref=dst, send_sem=send, recv_sem=recv, device_id=device, device_id_type=MESH
    )


def greet(devices):
    barrier = pltpu.get_barrier_semaphore()
    for device in devices:
        pl.semaphore_signal(barrier, inc=1, device_id=device, device_id_type=MESH)
    pl.semaphore_wait(barrier, len(devices))


def pair_indices(removed_s, pair):
    return [removed_s[pair * 16 + j] for j in range(16)]


def index_rows(indices, lanes):
    row = lax.broadcasted_iota(jnp.int32, (16, lanes), 0)
    out = jnp.full((16, lanes), -1, jnp.int32)
    for j, r in enumerate(indices):
        out = jnp.where(row == j, r, out)
    return out


def dot_nt(a, b):
    return lax.dot_general(a, b, (((1,), (1,)), ((), ())), preferred_element_type=F32)


def ranks(indices, first, offset, lanes, rows=16):
    lane = lax.broadcasted_iota(jnp.int32, (rows, lanes), 1) + (first + offset)
    below = jnp.zeros((rows, lanes), jnp.int32)
    gone = jnp.zeros((rows, lanes), jnp.int32)
    for r in indices:
        mine = jnp.where(r >= first, 1, 0)
        below = below + jnp.where(r < lane, mine, 0)
        gone = gone + jnp.where(r == lane, 1, 0)
    return jnp.where(gone > 0, -1, lane - first - below)


def split(value):
    high = value.astype(BF)
    return high, (value - high.astype(F32)).astype(BF)


def dot2(pair, b):
    return dot(pair[0], b) + dot(pair[1], b)


def dot3(a, b):
    return dot(a[0], b[0]) + (dot(a[0], b[1]) + dot(a[1], b[0]))


def newton(xy, between):
    n = HALF
    eye = lax.broadcasted_iota(jnp.int32, (n, n), 0) == lax.broadcasted_iota(jnp.int32, (n, n), 1)
    square = xy[n:, :]
    bound = jnp.max(jnp.sum(jnp.abs(square), axis=0, keepdims=True), axis=1, keepdims=True)
    inverse_bound = 1.0 / bound
    low = 0.5 * inverse_bound
    xy[n:, :] = square * inverse_bound
    for step in range(STEPS):
        middle = 0.5 * (1.0 + low)
        gain = 1.0 / (middle * middle)
        factor = (jnp.where(eye, 2.0 * middle, 0.0) - xy[n:, :]) * gain
        right = split(factor)
        if step == 0:
            xy[n:, :] = dot3(split(xy[n:, :]), right)
            xy[:n, :] = factor * inverse_bound
        elif step < STEPS - 1:
            xy[...] = dot3(split(xy[...]), right)
        else:
            xy[:n, :] = dot3(split(xy[:n, :]), right)
        low = low * gain
        between(step)
    xy[:n, :] = xy[:n, :] * (2.0 / (1.0 + low))


def prune_kernel(
    removed_s, tok_h, gate_h, up_h, down_h, hess_h, damp_h, removed_h,
    pruned_o, mixed_o,
    tok_in, down, damp, removed_v, hbuf, weight,
    tok_o, l_o, s_o, hkr_o, slabd_o, slabh_o,
    lpad, spad, l_rx, s_rx, slabd_tx, slabh_tx,
    lhs, pre, pre_tx, pre_rx, pre_own, hid,
    xy, inv, rows, corr, slabc,
    ptx, prx, own, x2, xa, xb, xtx, xrx, ztx, zrx, fin, frx,
    load_s, hess_s, pair_s, pair_r, sc_s, sc_r, y_s, y_r, z_s, z_r, x_s, x_r, c_s, c_r, sl_s, sl_r,
    ps_s, ps_r, h_s, h_r,
    p_s, p_r, a_s, a_r, e_s, e_r, w_s, w_r, f_s, f_r, packed_v, out_s,
):
    x, z, c, d = place()
    other = 1 - c
    pair = x * NZ + z
    first = (pair * 2 + c) * WIDTH
    quarter = FF // 4

    def load(src, dst, sem):
        copy = pltpu.make_async_copy(src, dst, sem)
        copy.start()
        return copy

    tok_load = load(tok_h, tok_in, load_s.at[0])
    removed_load = load(removed_h, removed_v, load_s.at[1])
    damp_load = load(damp_h, damp, load_s.at[2])
    hess_loads = [load(hess_h.at[:, pl.ds(g * quarter, quarter)], hbuf.at[g], hess_s.at[g]) for g in range(4)]
    down_load = load(down_h, down, load_s.at[3])
    gate_load = load(gate_h, weight.at[pl.ds(0, WIDTH)], load_s.at[4])
    up_load = load(up_h, weight.at[pl.ds(WIDTH, WIDTH)], load_s.at[5])

    partner = at(x, z, other, d)
    right, left = at((x + 1) % NX, z, c, d), at((x + 3) % NX, z, c, d)
    ydev = [at(x, z, c, (d + k) % NY) for k in range(1, NY)]
    ycross = [at(x, z, other, (d + k) % NY) for k in range(1, NY)]
    zdev = [at(x, (z + k) % NZ, c, d) for k in range(1, NZ)]
    greet([partner, right, left] + ydev + ycross + zdev)
    pending = []

    def send(src, dst, s, r, device):
        copy = remote(src, dst, s, r, device)
        copy.start()
        pending.append(copy)
        return copy

    def arrived(copies):
        for copy in copies:
            copy.wait_recv()

    def z_sends(array, n):
        here = array.at[c, x, z]
        return [send(here, here, z_s.at[n, k], z_r.at[n, k], zdev[k]) for k in range(NZ - 1)]

    def x_sends(array, n):
        here = array.at[c, x]
        return [
            send(here, here, x_s.at[n, 0], x_r.at[n, 0], right),
            send(here, here, x_s.at[n, 1], x_r.at[n, 1], left),
        ]

    def x_forwards(array, n):
        low = array.at[c, (x + 3) % NX, pl.ds(0, 4)]
        high = array.at[c, (x + 1) % NX, pl.ds(4, 4)]
        return [
            send(low, low, x_s.at[n, 2], x_r.at[n, 2], right),
            send(high, high, x_s.at[n, 3], x_r.at[n, 3], left),
        ]

    def core_send(array, n, k):
        here = array.at[c, (x + k) % NX]
        return send(here, here, c_s.at[n, k], c_r.at[n, k], partner)

    tok_load.wait()
    tok = tok_in[...].astype(F32)
    for h in range(2):
        cols = slice(h * 512, h * 512 + 512)
        tok_o[h, c, x, z] = jnp.concatenate([tok[:, :1024][:, cols], tok[:, 1024:][:, cols]], axis=0).astype(BF)
    tok_z = [z_sends(tok_o.at[h], 2 * h) for h in range(2)]

    indices = pair_indices(removed_s, pair)
    removed_load.wait()
    chunk = quarter // 4
    lane = lax.broadcasted_iota(jnp.int32, (1, 128), 1)
    channel = lax.broadcasted_iota(jnp.int32, (chunk, 128), 0)
    for g in range(4):
        hess_loads[g].wait()
        wanted = removed_v[g : g + 1, :] - (g * quarter + (lane // 32) * chunk)
        hot = jnp.where(channel == wanted, 1.0, 0.0).astype(BF)
        total = jnp.zeros((BLOCK, 128), F32)
        for q in range(4):
            part = dot(hbuf[g, :, q * chunk : (q + 1) * chunk], hot)
            total = jnp.where(lane // 32 == q, part, total)
        hkr_o[d, :, g * 128 : (g + 1) * 128] = total.astype(BF)
    rows104 = index_rows(indices, BLOCK)
    lane104 = lax.broadcasted_iota(jnp.int32, (16, BLOCK), 1)
    block_first = first + d * BLOCK
    pick104 = jnp.where(lane104 + block_first == rows104, 1.0, 0.0)
    own_rows = dot(pick104.astype(BF), hkr_o[d]).astype(BF)
    damp_load.wait()
    lane128 = lax.broadcasted_iota(jnp.int32, (16, 128), 1)
    row128 = lax.broadcasted_iota(jnp.int32, (16, 128), 0)
    found = jnp.zeros((16, 128), F32)
    for j, r in enumerate(indices):
        line = damp[pl.ds(r // 128, 1), :]
        here = jnp.where(r >= block_first, jnp.where(r < block_first + BLOCK, j, -1), -1)
        found = jnp.where(row128 == here, jnp.where(lane128 == r % 128, line, 0.0), found)
    damped = jnp.sum(found, axis=1, keepdims=True)
    high = damped.astype(BF).astype(F32)
    extra = jnp.where(lane128 == 0, high, jnp.where(lane128 == 1, damped - high, 0.0)).astype(BF)
    for half in range(2):
        spad[half, :, :256] = own_rows[:, half * 256 : (half + 1) * 256]
        spad[half, :, 256:] = extra
    s_sends = []
    for k in range(NY - 1):
        s_sends.append(send(spad.at[c], s_rx.at[k], sc_s.at[k], sc_r.at[k], ydev[k]))
        s_sends.append(send(spad.at[other], s_rx.at[3 + k], sc_s.at[3 + k], sc_r.at[3 + k], ycross[k]))
    s_sends.append(send(spad.at[other], s_rx.at[6], sc_s.at[6], sc_r.at[6], partner))
    h_sends = [send(hkr_o.at[d], hkr_o.at[d], y_s.at[k], y_r.at[k], ydev[k]) for k in range(NY - 1)]

    down_load.wait()
    rows416 = index_rows(indices, WIDTH)
    lane416 = lax.broadcasted_iota(jnp.int32, (16, WIDTH), 1)
    pick = jnp.where(lane416 + first == rows416, 1.0, 0.0).astype(BF)
    lost = dot(pick, down[...]).astype(BF)
    lpad[0] = lost[:, :1024]
    lpad[1] = lost[:, 1024:]
    l_pair = send(lpad.at[other], l_rx, pair_s.at[0], pair_r.at[0], partner)
    row16 = lax.broadcasted_iota(jnp.int32, (16, WIDTH), 0)
    target = jnp.where(row16 < 8, row16 + (1 - c) * KEPT, -7)
    slab_pick = jnp.where(ranks(indices, first, 0, WIDTH) == target, 1.0, 0.0)
    slabd_tx[...] = dot(slab_pick.astype(BF), down[...]).astype(BF)
    slabd = send(slabd_tx, slabd_o, sl_s.at[0], sl_r.at[0], partner)

    arrived(s_sends)
    total = spad[c].astype(F32)
    for k in range(7):
        total = total + s_rx[k].astype(F32)
    s_o[c, x, z] = total.astype(BF)
    s_z = z_sends(s_o, 3)
    arrived([l_pair])
    l_o[c, x, z] = lpad[c] + l_rx[...]
    tok_x = []
    for h in range(2):
        arrived(tok_z[h])
        tok_x.append(x_sends(tok_o.at[h], 2 * h))
    tok_c = {0: [core_send(tok_o.at[h], 2 * h, 0) for h in range(2)]}
    l_z = z_sends(l_o, 1)
    arrived(s_z)
    s_x = x_sends(s_o, 3)
    s_c = [core_send(s_o, 3, 0)]

    partials = {}

    def preact(k):
        arrived(tok_c[k])
        b = (x + k) % NX
        for core in range(2):
            for h in range(2):
                value = tok_o[h, core, b].astype(F32)
                cols = slice(h * 512, h * 512 + 512)
                lhs[0, core * 64 : core * 64 + 64, cols] = value[:, :8].reshape(64, 512).astype(BF)
                lhs[1, core * 64 : core * 64 + 64, cols] = value[:, 8:].reshape(64, 512).astype(BF)
        pre[...] = dot_nt(lhs[0], weight[:, :1024]) + dot_nt(lhs[1], weight[:, 1024:])
        sends = []
        for m in range(NY - 1):
            part = pl.ds(pl.multiple_of(((d + 1 + m) % NY) * 32, 32), 32)
            pre_tx[k, m] = pre[part, :].astype(BF)
            sends.append(send(pre_tx.at[k, m], pre_rx.at[k, m], ps_s.at[k, m], ps_r.at[k, m], ydev[m]))
        pre_own[k] = pre[pl.ds(pl.multiple_of(d * 32, 32), 32), :]
        partials[k] = sends

    shares = {}

    def gated(k):
        arrived(partials[k])
        value = pre_own[k]
        for m in range(NY - 1):
            value = value + pre_rx[k, m].astype(F32)
        gate, up = value[:, :WIDTH], value[:, WIDTH:]
        lane = lax.broadcasted_iota(jnp.int32, (32, WIDTH), 1) + first
        hidden = gate / (1.0 + jnp.exp(-gate)) * up
        for r in indices:
            hidden = jnp.where(lane == r, 0.0, hidden)
        hid[k, d] = hidden.astype(BF)
        here = hid.at[k, d]
        shares[k] = [send(here, here, h_s.at[k, m], h_r.at[k, m], ydev[m]) for m in range(NY - 1)]

    gate_load.wait()
    up_load.wait()
    preact(0)
    tok_f = []
    tok_c[1], tok_c[3] = [], []
    for h in range(2):
        arrived(tok_x[h])
        tok_f.append(x_forwards(tok_o.at[h], 2 * h))
        tok_c[1].append(core_send(tok_o.at[h], 2 * h, 1))
        tok_c[3].append(core_send(tok_o.at[h], 2 * h, 3))
    arrived(s_x)
    s_f = x_forwards(s_o, 3)
    s_c += [core_send(s_o, 3, 1), core_send(s_o, 3, 3)]
    preact(1)
    preact(3)
    arrived(l_z)
    later = {"x": x_sends(l_o, 1), "c": [core_send(l_o, 1, 0)]}
    arrived(s_f)
    s_c.append(core_send(s_o, 3, 2))

    def tokens_last():
        tok_c[2] = []
        for h in range(2):
            arrived(tok_f[h])
            tok_c[2].append(core_send(tok_o.at[h], 2 * h, 2))

    def lost_forward():
        arrived(later["x"])
        later["f"] = x_forwards(l_o, 1)
        later["c"] += [core_send(l_o, 1, 1), core_send(l_o, 1, 3)]

    def lost_last():
        arrived(later["f"])
        later["c"].append(core_send(l_o, 1, 2))

    def gather_rows():
        arrived(h_sends)
        slab = jnp.zeros((16, REM), F32)
        for k in range(NY):
            mine = ranks(indices, first, k * BLOCK, BLOCK) == target[:, :BLOCK]
            slab = slab + dot(jnp.where(mine, 1.0, 0.0).astype(BF), hkr_o[k])
            rows[k * BLOCK : (k + 1) * BLOCK] = hkr_o[k].astype(F32)
        slabh_tx[...] = slab.astype(BF)
        later["s"] = send(slabh_tx, slabh_o, sl_s.at[1], sl_r.at[1], partner)

    eye = lax.broadcasted_iota(jnp.int32, (HALF, HALF), 0) == lax.broadcasted_iota(jnp.int32, (HALF, HALF), 1)

    def s_block(i, j):
        return s_o[j, 2 * i : 2 * i + 2, :, :, :256].reshape(HALF, 256)

    def diagonal(i):
        damping = s_o[0, 2 * i : 2 * i + 2, :, :, 256:].reshape(HALF, 128).astype(F32)
        return jnp.where(eye, damping[:, 0:1] + damping[:, 1:2], 0.0)

    tokens_last()
    arrived(s_c)
    xy[HALF:, :] = s_block(0, 0).astype(F32) + diagonal(0)
    tasks = {1: [lambda: preact(2)], 4: [lambda: gated(0)]}
    more_tasks = {
        0: [lost_forward, lambda: gated(1)], 1: [lambda: gated(3)], 5: [lambda: gated(2)], 6: [lost_last],
    }

    def between(plan):
        def run(step):
            for task in plan.get(step, []):
                task()

        return run

    newton(xy, between(tasks))
    gather_rows()
    inv[...] = xy[:HALF, :]
    a_inv = split(inv[...])
    b_block = s_block(0, 1)
    v = dot(s_block(1, 0), a_inv[0]) + dot(s_block(1, 0), a_inv[1])
    xy[HALF:, :] = s_block(1, 1).astype(F32) + diagonal(1) - dot2(split(v), b_block)
    newton(xy, between(more_tasks))
    e_inv = split(xy[:HALF, :])
    arrived([slabd, later["s"]])
    rows[WIDTH:] = slabh_o[...].astype(F32)
    q = dot(rows[:, :HALF].astype(BF), a_inv[0]) + dot(rows[:, :HALF].astype(BF), a_inv[1])
    u = rows[:, HALF:] - dot2(split(q), b_block)
    second = dot3(split(u), e_inv)
    pair_first = split(q - dot3(split(second), split(v)))
    pair_second = split(second)
    arrived(later["c"])
    lost_all = [l_o[h].reshape(REM, 1024) for h in range(2)]
    for half in range(2):
        cols = pl.ds(half * 1024, 1024)
        change = dot2(pair_first, lost_all[half][:HALF]) + dot2(pair_second, lost_all[half][HALF:])
        corr[:, cols] = (down[:, cols].astype(F32) - change[:WIDTH]).astype(BF)
        slabc[:, cols] = (slabd_o[:, cols].astype(F32) - change[WIDTH:]).astype(BF)

    scale = FF ** (-0.5)
    order = (2, 1, 3, 0)
    low, top = pl.ds(0, 64), pl.ds(64, 64)
    pairs, to_right, to_left, plain, summed = {}, [], [], [], []
    for k in order:
        arrived(shares[k])

    def product(k, core, h):
        cols = pl.ds(pl.multiple_of(core * 1024 + h * 512, 512), 512)
        return dot(hid[k].reshape(128, WIDTH), corr[:, cols]) * scale

    for h in range(2):
        for k in order:
            ptx[h, k] = product(k, other, h).astype(BF)
            pairs[h, k] = send(ptx.at[h, k], prx.at[h, k], p_s.at[h, k], p_r.at[h, k], partner)
        for k in order:
            own[h, k] = product(k, c, h)
        arrived([pairs[h, 2]])
        x2[h] = (own[h, 2] + prx[h, 2].astype(F32)).astype(BF)
        to_right.append(send(x2.at[h, low], xa.at[h], a_s.at[h, 0], a_r.at[h, 0], right))
        to_left.append(send(x2.at[h, top], xb.at[h], a_s.at[h, 1], a_r.at[h, 1], left))
        arrived([pairs[h, 1]])
        own[h, 1] = own[h, 1] + prx[h, 1].astype(F32)
        xtx[h, 0, 64:] = own[h, 1, 64:].astype(BF)
        here, there = xtx.at[h, 0, top], xrx.at[h, 0, top]
        plain.append([send(here, there, e_s.at[h, 0], e_r.at[h, 0], right)])
        arrived([pairs[h, 3]])
        own[h, 3] = own[h, 3] + prx[h, 3].astype(F32)
        xtx[h, 1, :64] = own[h, 3, :64].astype(BF)
        here, there = xtx.at[h, 1, low], xrx.at[h, 1, low]
        plain[h].append(send(here, there, e_s.at[h, 1], e_r.at[h, 1], left))

    even = (pair * 2 + 1) * WIDTH
    even_kept = WIDTH
    for r in indices:
        even_kept = even_kept - jnp.where(r < even, 1, 0)
    rank = ranks(indices, first, 0, WIDTH, 8)
    goal = jnp.where(rank < 0, -1, rank + c * (even_kept - KEPT))[:1]
    row = lax.broadcasted_iota(jnp.int32, (KEPT, WIDTH), 0)
    pack = jnp.where(row == goal, 1.0, 0.0).astype(BF)
    lane = lax.broadcasted_iota(jnp.int32, (8, 16), 1)
    from_odd = even_kept + lane
    from_even = jnp.where(KEPT + lane < even_kept, lane, -1)
    slab_goal = jnp.where(lane < 8, jnp.where(c == 0, from_odd, from_even), -1)[:1]
    row = lax.broadcasted_iota(jnp.int32, (KEPT, 16), 0)
    slab_pack = jnp.where(row == slab_goal, 1.0, 0.0).astype(BF)

    stored = []

    def packed(half):
        cols = pl.ds(half * 1024, 1024)
        packed_v[half] = (dot(pack, corr[:, cols]) + dot(slab_pack, slabc[:, cols])).astype(BF)
        for k in range(4):
            there = pruned_o.at[:, pl.ds(half * 1024 + k * 256, 256)]
            copy = pltpu.make_async_copy(packed_v.at[half, :, pl.ds(k * 256, 256)], there, out_s.at[half, k])
            copy.start()
            stored.append(copy)

    for h in range(2):
        arrived([to_right[h]])
        xtx[h, 0, :64] = (own[h, 1, :64] + xa[h].astype(F32)).astype(BF)
        here, there = xtx.at[h, 0, low], xrx.at[h, 0, low]
        summed.append([send(here, there, e_s.at[h, 2], e_r.at[h, 2], right)])
        arrived([to_left[h]])
        xtx[h, 1, 64:] = (own[h, 3, 64:] + xb[h].astype(F32)).astype(BF)
        here, there = xtx.at[h, 1, top], xrx.at[h, 1, top]
        summed[h].append(send(here, there, e_s.at[h, 3], e_r.at[h, 3], left))
        packed(h)

    def z_rows(h, k):
        start = pl.multiple_of(((z + k) % NZ) * 8, 8)
        return jnp.concatenate([own[h, 0, pl.ds(start, 8)], own[h, 0, pl.ds(64 + start, 8)]], axis=0)

    zs = {}
    for h in range(2):
        arrived([pairs[h, 0]])
        total = own[h, 0] + prx[h, 0].astype(F32)
        arrived(plain[h] + summed[h])
        own[h, 0] = total + xrx[h, 0].astype(F32) + xrx[h, 1].astype(F32)
        for k in range(1, NZ):
            ztx[h, k - 1] = z_rows(h, k).astype(BF)
            here, there = ztx.at[h, k - 1], zrx.at[h, k - 1]
            zs[h, k] = send(here, there, w_s.at[h, k - 1], w_r.at[h, k - 1], zdev[k - 1])
    for h in range(2):
        total = z_rows(h, 0)
        for k in range(1, NZ):
            arrived([zs[h, k]])
            total = total + zrx[h, k - 1].astype(F32)
        fin[0, :, h * 512 : h * 512 + 512] = total[:8]
        fin[1, :, h * 512 : h * 512 + 512] = total[8:]
    last = send(fin.at[other], frx, f_s.at[0], f_r.at[0], partner)
    mine = pl.ds(pl.multiple_of(c * 1024, 1024), 1024)
    theirs = pl.ds(pl.multiple_of(other * 1024, 1024), 1024)
    mixed_o[:, mine] = fin[c].astype(BF)
    arrived([last])
    mixed_o[:, theirs] = frx[...].astype(BF)
    for copy in stored:
        copy.wait()
    for copy in pending:
        copy.wait_send()


def hand_over_kernel(pruned, mixed, pruned_o, mixed_o, pruned_v, mixed_v, in_s, out_s):
    parts = []
    for k in range(PIECES):
        cols = pl.ds(k * (2048 // PIECES), 2048 // PIECES)
        parts.append((pruned.at[:, cols], pruned_v.at[k], pruned_o.at[:, cols]))
    parts.append((mixed, mixed_v, mixed_o))
    arriving = [pltpu.make_async_copy(src, mid, in_s.at[k]) for k, (src, mid, _) in enumerate(parts)]
    leaving = [pltpu.make_async_copy(mid, dst, out_s.at[k]) for k, (_, mid, dst) in enumerate(parts)]
    for copy in arriving:
        copy.start()
    for into, copy in zip(arriving, leaving):
        into.wait()
        copy.start()
    for copy in leaving:
        copy.wait()


def dma(*shape):
    return pltpu.SemaphoreType.DMA(shape)


def vmem():
    return pl.BlockSpec(memory_space=pltpu.VMEM)


def hbm():
    return pl.BlockSpec(memory_space=pl.ANY)


def out(*shape):
    return jax.ShapeDtypeStruct(shape, BF)


def shards(tokens, gate_weight, up_weight, down_weight, inverse_hessian, damping, removed):
    def bf(*shape):
        return pltpu.VMEM(shape, BF)

    def f32(*shape):
        return pltpu.VMEM(shape, F32)

    pruned, mixed = pl.pallas_call(
        prune_kernel,
        out_shape=(out(KEPT, 2048), out(8, 2048)),
        in_specs=[pl.BlockSpec(memory_space=pltpu.SMEM)] + [hbm()] * 7,
        out_specs=(hbm(), vmem()),
        scratch_shapes=[
            bf(8, 2048), bf(WIDTH, 2048), f32(FF // 128, 128), pltpu.VMEM((4, 128), jnp.int32),
            bf(4, BLOCK, FF // 4), bf(2 * WIDTH, 2048),
            bf(2, 2, NX, NZ, 16, 512), bf(2, NX, NZ, 16, 1024), bf(2, NX, NZ, 16, 384),
            bf(NY, BLOCK, REM), bf(16, 2048), bf(16, REM),
            bf(2, 16, 1024), bf(2, 16, 384), bf(16, 1024), bf(7, 16, 384), bf(16, 2048), bf(16, REM),
            bf(2, 128, 1024), f32(128, 2 * WIDTH), bf(4, 3, 32, 2 * WIDTH), bf(4, 3, 32, 2 * WIDTH),
            f32(4, 32, 2 * WIDTH), bf(4, NY, 32, WIDTH),
            f32(2 * HALF, HALF), f32(HALF, HALF), f32(WIDTH + 16, REM), bf(WIDTH, 2048), bf(16, 2048),
            bf(2, 4, 128, 512), bf(2, 4, 128, 512), f32(2, 4, 128, 512), bf(2, 128, 512), bf(2, 64, 512), bf(2, 64, 512),
            bf(2, 2, 128, 512), bf(2, 2, 128, 512), bf(2, 7, 16, 512), bf(2, 7, 16, 512), f32(2, 8, 1024), f32(8, 1024),
            dma(6), dma(4), dma(1), dma(1), dma(7), dma(7), dma(3), dma(3), dma(4, 7), dma(4, 7),
            dma(4, 4), dma(4, 4), dma(4, 4), dma(4, 4), dma(2), dma(2),
            dma(4, 3), dma(4, 3), dma(4, 3), dma(4, 3),
            dma(2, 4), dma(2, 4), dma(2, 2), dma(2, 2), dma(2, 4), dma(2, 4), dma(2, 7), dma(2, 7), dma(1), dma(1),
            bf(2, KEPT, 1024), dma(2, 4),
        ],
        compiler_params=pltpu.CompilerParams(
            collective_id=1, has_side_effects=True, vmem_limit_bytes=VMEM_LIMIT
        ),
        name="prune",
    )(
        removed, tokens, gate_weight.T, up_weight.T, down_weight, inverse_hessian,
        damping.reshape(FF // 128, 128), removed.reshape(4, 128),
    )
    return pl.pallas_call(
        hand_over_kernel,
        out_shape=(out(KEPT, 2048), out(8, 2048)),
        in_specs=[hbm(), hbm()],
        out_specs=(hbm(), hbm()),
        scratch_shapes=[
            bf(PIECES, KEPT, 2048 // PIECES), bf(8, 2048), dma(PIECES + 1), dma(PIECES + 1),
        ],
        compiler_params=pltpu.CompilerParams(vmem_limit_bytes=VMEM_LIMIT),
        name="hand_over",
    )(pruned, mixed)


def solution(mesh):
    in_specs = (
        P("tensor", "dp"),
        P("dp", "tensor"),
        P("dp", "tensor"),
        P("tensor", "dp"),
        P(("tensor", "dp"), None),
        P(),
        P(),
    )
    out_specs = (P("tensor", "dp"), P("tensor", "dp"))
    return jax.shard_map(shards, mesh=mesh, in_specs=in_specs, out_specs=out_specs, check_vma=False)
```

```python
import jax
import jax.numpy as jnp
from jax import lax
from jax.experimental import pallas as pl
from jax.experimental.pallas import tpu as pltpu
from jax.sharding import PartitionSpec as P

MESH = pl.DeviceIdType.MESH
BF = jnp.bfloat16
F32 = jnp.float32
NX, NZ, NY = 4, 8, 4
WIDTH = 416
BLOCK = 104
KEPT = 408
FF = 26624
REM = 512
STEPS = 7
HALF = REM // 2
PIECES = 8
SPLIT = 4
VMEM_LIMIT = 56 * 1024 * 1024


def dot(a, b):
    return jnp.dot(a, b, preferred_element_type=F32)


def place():
    t = lax.axis_index("tensor")
    d = lax.axis_index("dp")
    return t // 16, (t // 2) % 8, t % 2, d


def at(x, z, c, d):
    return (x * 16 + z * 2 + c, d)


def remote(src, dst, send, recv, device):
    return pltpu.make_async_remote_copy(
        src_ref=src, dst_ref=dst, send_sem=send, recv_sem=recv, device_id=device, device_id_type=MESH
    )


def greet(devices):
    barrier = pltpu.get_barrier_semaphore()
    for device in devices:
        pl.semaphore_signal(barrier, inc=1, device_id=device, device_id_type=MESH)
    pl.semaphore_wait(barrier, len(devices))


def pair_indices(removed_s, pair):
    return [removed_s[pair * 16 + j] for j in range(16)]


def index_rows(indices, lanes):
    row = lax.broadcasted_iota(jnp.int32, (16, lanes), 0)
    out = jnp.full((16, lanes), -1, jnp.int32)
    for j, r in enumerate(indices):
        out = jnp.where(row == j, r, out)
    return out


def ranks(indices, first, offset, lanes, rows=16):
    lane = lax.broadcasted_iota(jnp.int32, (rows, lanes), 1) + (first + offset)
    below = jnp.zeros((rows, lanes), jnp.int32)
    gone = jnp.zeros((rows, lanes), jnp.int32)
    for r in indices:
        mine = jnp.where(r >= first, 1, 0)
        below = below + jnp.where(r < lane, mine, 0)
        gone = gone + jnp.where(r == lane, 1, 0)
    return jnp.where(gone > 0, -1, lane - first - below)


def split(value):
    high = value.astype(BF)
    return high, (value - high.astype(F32)).astype(BF)


def dot2(pair, b):
    return dot(pair[0], b) + dot(pair[1], b)


def dot3(a, b):
    return dot(a[0], b[0]) + (dot(a[0], b[1]) + dot(a[1], b[0]))


def newton(xy, between):
    n = HALF
    eye = lax.broadcasted_iota(jnp.int32, (n, n), 0) == lax.broadcasted_iota(jnp.int32, (n, n), 1)
    square = xy[n:, :]
    bound = jnp.max(jnp.sum(jnp.abs(square), axis=0, keepdims=True), axis=1, keepdims=True)
    inverse_bound = 1.0 / bound
    low = 0.9 * inverse_bound
    xy[n:, :] = square * inverse_bound
    for step in range(STEPS):
        middle = 0.5 * (1.0 + low)
        gain = 1.0 / (middle * middle)
        factor = (jnp.where(eye, 2.0 * middle, 0.0) - xy[n:, :]) * gain
        right = split(factor)
        if step == 0:
            xy[n:, :] = dot3(split(xy[n:, :]), right)
            xy[:n, :] = factor * inverse_bound
        elif step < STEPS - 1:
            xy[...] = dot3(split(xy[...]), right)
        else:
            xy[:n, :] = dot3(split(xy[:n, :]), right)
        low = low * gain
        between(step)
    xy[:n, :] = xy[:n, :] * (2.0 / (1.0 + low))


def prune_kernel(
    removed_s, tok_h, gate_h, up_h, down_h, hess_h, damp_h, removed_h,
    pruned_o, mixed_o,
    tok_in, down, damp, removed_v, hbuf, weight,
    tok_o, l_a, l_b, s_o, hkr_o, slabd_o, slabh_o,
    lpad, spad, l_rx, s_rx, slabd_tx, slabh_tx,
    lhs, pre, pre_tx, pre_rx, pre_own, hid,
    xy, inv, rows, corr, slabc,
    ptx, prx, own, x2, xa, xb, xtx, xrx, ztx, zrx,
    load_s, hess_s, pair_s, pair_r, sc_s, sc_r, y_s, y_r, z_s, z_r, x_s, x_r, c_s, c_r, sl_s, sl_r,
    ps_s, ps_r, h_s, h_r,
    p_s, p_r, a_s, a_r, e_s, e_r, w_s, w_r, packed_v, out_s, turned, lx_s, lx_r,
):
    x, z, c, d = place()
    other = 1 - c
    pair = x * NZ + z
    first = (pair * 2 + c) * WIDTH
    quarter = FF // 4

    def load(src, dst, sem):
        copy = pltpu.make_async_copy(src, dst, sem)
        copy.start()
        return copy

    tok_load = load(tok_h, tok_in, load_s.at[0])
    removed_load = load(removed_h, removed_v, load_s.at[1])
    damp_load = load(damp_h, damp, load_s.at[2])
    hess_loads = [load(hess_h.at[:, pl.ds(g * quarter, quarter)], hbuf.at[g], hess_s.at[g]) for g in range(4)]
    down_load = load(down_h, down, load_s.at[3])
    gate_load = load(gate_h, weight.at[pl.ds(0, WIDTH)], load_s.at[4])
    up_load = load(up_h, weight.at[pl.ds(WIDTH, WIDTH)], load_s.at[5])

    partner = at(x, z, other, d)
    right, left = at((x + 1) % NX, z, c, d), at((x + 3) % NX, z, c, d)
    ydev = [at(x, z, c, (d + k) % NY) for k in range(1, NY)]
    ycross = [at(x, z, other, (d + k) % NY) for k in range(1, NY)]
    across = at((x + 2) % NX, z, c, d)
    zdev = [at(x, (z + k) % NZ, c, d) for k in range(1, NZ)]
    greet([partner, right, left, across] + ydev + ycross + zdev)
    pending = []

    def send(src, dst, s, r, device):
        copy = remote(src, dst, s, r, device)
        copy.start()
        pending.append(copy)
        return copy

    def arrived(copies):
        for copy in copies:
            copy.wait_recv()

    def z_sends(array, n):
        here = array.at[c, x, z]
        return [send(here, here, z_s.at[n, k], z_r.at[n, k], zdev[k]) for k in range(NZ - 1)]

    def x_sends(array, n):
        here = array.at[c, x]
        return [
            send(here, here, x_s.at[n, 0], x_r.at[n, 0], right),
            send(here, here, x_s.at[n, 1], x_r.at[n, 1], left),
        ]

    def x_forwards(array, n):
        low = array.at[c, (x + 3) % NX, pl.ds(0, 4)]
        high = array.at[c, (x + 1) % NX, pl.ds(4, 4)]
        return [
            send(low, low, x_s.at[n, 2], x_r.at[n, 2], right),
            send(high, high, x_s.at[n, 3], x_r.at[n, 3], left),
        ]

    def core_send(array, n, k):
        here = array.at[c, (x + k) % NX]
        return send(here, here, c_s.at[n, k], c_r.at[n, k], partner)

    tok_load.wait()
    tok = tok_in[...].astype(F32)
    for h in range(2):
        cols = slice(h * 512, h * 512 + 512)
        tok_o[h, c, x, z] = jnp.concatenate([tok[:, :1024][:, cols], tok[:, 1024:][:, cols]], axis=0).astype(BF)
    tok_z = [z_sends(tok_o.at[h], 2 * h) for h in range(2)]

    indices = pair_indices(removed_s, pair)
    removed_load.wait()
    chunk = quarter // 4
    lane = lax.broadcasted_iota(jnp.int32, (1, 128), 1)
    channel = lax.broadcasted_iota(jnp.int32, (chunk, 128), 0)
    for g in range(4):
        hess_loads[g].wait()
        wanted = removed_v[g : g + 1, :] - (g * quarter + (lane // 32) * chunk)
        hot = jnp.where(channel == wanted, 1.0, 0.0).astype(BF)
        total = jnp.zeros((BLOCK, 128), F32)
        for q in range(4):
            part = dot(hbuf[g, :, q * chunk : (q + 1) * chunk], hot)
            total = jnp.where(lane // 32 == q, part, total)
        hkr_o[d, :, g * 128 : (g + 1) * 128] = total.astype(BF)
    rows104 = index_rows(indices, BLOCK)
    lane104 = lax.broadcasted_iota(jnp.int32, (16, BLOCK), 1)
    block_first = first + d * BLOCK
    pick104 = jnp.where(lane104 + block_first == rows104, 1.0, 0.0)
    own_rows = dot(pick104.astype(BF), hkr_o[d]).astype(BF)
    damp_load.wait()
    lane128 = lax.broadcasted_iota(jnp.int32, (16, 128), 1)
    row128 = lax.broadcasted_iota(jnp.int32, (16, 128), 0)
    found = jnp.zeros((16, 128), F32)
    for j, r in enumerate(indices):
        line = damp[pl.ds(r // 128, 1), :]
        here = jnp.where(r >= block_first, jnp.where(r < block_first + BLOCK, j, -1), -1)
        found = jnp.where(row128 == here, jnp.where(lane128 == r % 128, line, 0.0), found)
    damped = jnp.sum(found, axis=1, keepdims=True)
    high = damped.astype(BF).astype(F32)
    extra = jnp.where(lane128 == 0, high, jnp.where(lane128 == 1, damped - high, 0.0)).astype(BF)
    for half in range(2):
        spad[half, :, :256] = own_rows[:, half * 256 : (half + 1) * 256]
        spad[half, :, 256:] = extra
    s_sends = []
    for k in range(NY - 1):
        s_sends.append(send(spad.at[c], s_rx.at[k], sc_s.at[k], sc_r.at[k], ydev[k]))
        s_sends.append(send(spad.at[other], s_rx.at[3 + k], sc_s.at[3 + k], sc_r.at[3 + k], ycross[k]))
    s_sends.append(send(spad.at[other], s_rx.at[6], sc_s.at[6], sc_r.at[6], partner))
    h_sends = [send(hkr_o.at[d], hkr_o.at[d], y_s.at[k], y_r.at[k], ydev[k]) for k in range(NY - 1)]

    down_load.wait()
    rows416 = index_rows(indices, WIDTH)
    lane416 = lax.broadcasted_iota(jnp.int32, (16, WIDTH), 1)
    pick = jnp.where(lane416 + first == rows416, 1.0, 0.0).astype(BF)
    lost = dot(pick, down[...]).astype(BF)
    lpad[0] = lost[:, :1024]
    lpad[1] = lost[:, 1024:]
    l_pair = send(lpad.at[other], l_rx, pair_s.at[0], pair_r.at[0], partner)
    row16 = lax.broadcasted_iota(jnp.int32, (16, WIDTH), 0)
    target = jnp.where(row16 < 8, row16 + (1 - c) * KEPT, -7)
    slab_pick = jnp.where(ranks(indices, first, 0, WIDTH) == target, 1.0, 0.0)
    slabd_tx[...] = dot(slab_pick.astype(BF), down[...]).astype(BF)
    slabd = send(slabd_tx, slabd_o, sl_s.at[0], sl_r.at[0], partner)

    gate_load.wait()
    up_load.wait()
    for i in range(4):
        turned[512 * i : 512 * i + 512] = weight[:, 512 * i : 512 * i + 512].T
    arrived(s_sends)
    total = spad[c].astype(F32)
    for k in range(7):
        total = total + s_rx[k].astype(F32)
    s_o[c, x, z] = total.astype(BF)
    s_z = z_sends(s_o, 3)
    arrived([l_pair])
    value = lpad[c] + l_rx[...]
    l_a[c, x, z] = value[:, :512]
    l_b[c, z, x] = value[:, 512:]
    here = l_b.at[c, z, x]
    lb_x = [send(here, here, lx_s.at[k], lx_r.at[k], (right, across, left)[k]) for k in range(3)]
    tok_x = []
    for h in range(2):
        arrived(tok_z[h])
        tok_x.append(x_sends(tok_o.at[h], 2 * h))
    tok_c = {0: [core_send(tok_o.at[h], 2 * h, 0) for h in range(2)]}
    l_z = z_sends(l_a, 1)
    arrived(lb_x)
    here = l_b.at[c, z]
    lb_z = [send(here, here, z_s.at[4, k], z_r.at[4, k], zdev[k]) for k in range(NZ - 1)]
    arrived(s_z)
    s_x = x_sends(s_o, 3)
    s_c = [core_send(s_o, 3, 0)]

    partials = {}

    def preact(k):
        arrived(tok_c[k])
        b = (x + k) % NX
        for core in range(2):
            for h in range(2):
                value = tok_o[h, core, b].astype(F32)
                cols = slice(h * 512, h * 512 + 512)
                lhs[0, core * 64 : core * 64 + 64, cols] = value[:, :8].reshape(64, 512).astype(BF)
                lhs[1, core * 64 : core * 64 + 64, cols] = value[:, 8:].reshape(64, 512).astype(BF)
        pre[...] = dot(lhs[0], turned[:1024]) + dot(lhs[1], turned[1024:])
        sends = []
        for m in range(NY - 1):
            part = pl.ds(pl.multiple_of(((d + 1 + m) % NY) * 32, 32), 32)
            pre_tx[k, m] = pre[part, :].astype(BF)
            sends.append(send(pre_tx.at[k, m], pre_rx.at[k, m], ps_s.at[k, m], ps_r.at[k, m], ydev[m]))
        pre_own[k] = pre[pl.ds(pl.multiple_of(d * 32, 32), 32), :]
        partials[k] = sends

    shares = {}

    def gated(k):
        arrived(partials[k])
        value = pre_own[k]
        for m in range(NY - 1):
            value = value + pre_rx[k, m].astype(F32)
        gate, up = value[:, :WIDTH], value[:, WIDTH:]
        lane = lax.broadcasted_iota(jnp.int32, (32, WIDTH), 1) + first
        hidden = gate / (1.0 + jnp.exp(-gate)) * up
        for r in indices:
            hidden = jnp.where(lane == r, 0.0, hidden)
        hid[d // 2, k, d % 2] = hidden.astype(BF)
        here = hid.at[d // 2, k, d % 2]
        shares[k] = [send(here, here, h_s.at[k, m], h_r.at[k, m], ydev[m]) for m in range(NY - 1)]

    preact(0)
    tok_f = []
    tok_c[1], tok_c[3] = [], []
    for h in range(2):
        arrived(tok_x[h])
        tok_f.append(x_forwards(tok_o.at[h], 2 * h))
        tok_c[1].append(core_send(tok_o.at[h], 2 * h, 1))
        tok_c[3].append(core_send(tok_o.at[h], 2 * h, 3))
    arrived(s_x)
    s_f = x_forwards(s_o, 3)
    s_c += [core_send(s_o, 3, 1), core_send(s_o, 3, 3)]
    preact(1)
    arrived(s_f)
    s_c.append(core_send(s_o, 3, 2))
    preact(3)
    arrived(l_z)
    later = {"x": x_sends(l_a, 1), "c": [core_send(l_a, 1, 0)]}

    def tokens_last():
        tok_c[2] = []
        for h in range(2):
            arrived(tok_f[h])
            tok_c[2].append(core_send(tok_o.at[h], 2 * h, 2))

    def lost_forward():
        arrived(later["x"])
        later["f"] = x_forwards(l_a, 1)
        later["c"] += [core_send(l_a, 1, 1), core_send(l_a, 1, 3)]

    def lost_other():
        arrived(lb_z)
        later["c"].append(send(l_b.at[c], l_b.at[c], c_s.at[4, 0], c_r.at[4, 0], partner))

    def lost_last():
        arrived(later["f"])
        later["c"].append(core_send(l_a, 1, 2))

    def gather_rows():
        arrived(h_sends)
        slab = jnp.zeros((16, REM), F32)
        for k in range(NY):
            mine = ranks(indices, first, k * BLOCK, BLOCK) == target[:, :BLOCK]
            slab = slab + dot(jnp.where(mine, 1.0, 0.0).astype(BF), hkr_o[k])
            rows[k * BLOCK : (k + 1) * BLOCK] = hkr_o[k].astype(F32)
        slabh_tx[...] = slab.astype(BF)
        later["s"] = send(slabh_tx, slabh_o, sl_s.at[1], sl_r.at[1], partner)

    eye = lax.broadcasted_iota(jnp.int32, (HALF, HALF), 0) == lax.broadcasted_iota(jnp.int32, (HALF, HALF), 1)

    def s_block(i, j):
        return s_o[j, 2 * i : 2 * i + 2, :, :, :256].reshape(HALF, 256)

    def diagonal(i):
        damping = s_o[0, 2 * i : 2 * i + 2, :, :, 256:].reshape(HALF, 128).astype(F32)
        return jnp.where(eye, damping[:, 0:1] + damping[:, 1:2], 0.0)

    tokens_last()
    arrived(s_c)
    xy[HALF:, :] = s_block(0, 0).astype(F32) + diagonal(0)
    tasks = {1: [lambda: preact(2)], 4: [lambda: gated(0)], 6: [lost_forward, lambda: gated(1)]}
    more_tasks = {
        0: [lambda: gated(3)], 2: [lost_other], 3: [lambda: gated(2)], 5: [lost_last],
    }

    def between(plan):
        def run(step):
            for task in plan.get(step, []):
                task()

        return run

    newton(xy, between(tasks))
    gather_rows()
    inv[...] = xy[:HALF, :]
    a_inv = split(inv[...])
    b_block = s_block(0, 1)
    v = dot(s_block(1, 0), a_inv[0]) + dot(s_block(1, 0), a_inv[1])
    xy[HALF:, :] = s_block(1, 1).astype(F32) + diagonal(1) - dot2(split(v), b_block)
    newton(xy, between(more_tasks))
    e_inv = split(xy[:HALF, :])
    arrived([slabd, later["s"]])
    rows[WIDTH:] = slabh_o[...].astype(F32)
    q = dot(rows[:, :HALF].astype(BF), a_inv[0]) + dot(rows[:, :HALF].astype(BF), a_inv[1])
    u = rows[:, HALF:] - dot2(split(q), b_block)
    second = dot3(split(u), e_inv)
    coef = [(q - dot3(split(second), split(v))).astype(BF), second.astype(BF)]
    arrived(later["c"])
    for half in range(2):
        first_rows = l_a[half].reshape(REM, 512)
        other_rows = jnp.concatenate([l_b[half, :, k].reshape(128, 512) for k in range(NX)], axis=0)
        for piece, lost_rows in enumerate((first_rows, other_rows)):
            cols = pl.ds(half * 1024 + piece * 512, 512)
            change = dot(coef[0], lost_rows[:HALF]) + dot(coef[1], lost_rows[HALF:])
            corr[:, cols] = (down[:, cols].astype(F32) - change[:WIDTH]).astype(BF)
            slabc[:, cols] = (slabd_o[:, cols].astype(F32) - change[WIDTH:]).astype(BF)

    wide = 2048 // SPLIT
    scale = FF ** (-0.5)
    order = (2, 1, 3, 0)
    low, top = pl.ds(0, 32), pl.ds(32, 32)
    pairs, to_right, to_left, plain, summed = {}, [], [], [], []
    for k in order:
        arrived(shares[k])

    def product(core, h):
        cols = pl.ds(h * wide, wide)
        return dot(hid[core].reshape(256, WIDTH), corr[:, cols]) * scale

    for h in range(SPLIT):
        ptx[h] = product(other, h).reshape(4, 64, wide).astype(BF)
        for k in order:
            pairs[h, k] = send(ptx.at[h, k], prx.at[h, k], p_s.at[h, k], p_r.at[h, k], partner)
        own[h] = product(c, h).reshape(4, 64, wide)
        arrived([pairs[h, 2]])
        x2[h] = (own[h, 2] + prx[h, 2].astype(F32)).astype(BF)
        to_right.append(send(x2.at[h, low], xa.at[h], a_s.at[h, 0], a_r.at[h, 0], right))
        to_left.append(send(x2.at[h, top], xb.at[h], a_s.at[h, 1], a_r.at[h, 1], left))
        arrived([pairs[h, 1]])
        own[h, 1] = own[h, 1] + prx[h, 1].astype(F32)
        xtx[h, 0, 32:] = own[h, 1, 32:].astype(BF)
        here, there = xtx.at[h, 0, top], xrx.at[h, 0, top]
        plain.append([send(here, there, e_s.at[h, 0], e_r.at[h, 0], right)])
        arrived([pairs[h, 3]])
        own[h, 3] = own[h, 3] + prx[h, 3].astype(F32)
        xtx[h, 1, :32] = own[h, 3, :32].astype(BF)
        here, there = xtx.at[h, 1, low], xrx.at[h, 1, low]
        plain[h].append(send(here, there, e_s.at[h, 1], e_r.at[h, 1], left))

    even = (pair * 2 + 1) * WIDTH
    even_kept = WIDTH
    for r in indices:
        even_kept = even_kept - jnp.where(r < even, 1, 0)
    rank = ranks(indices, first, 0, WIDTH, 8)
    goal = jnp.where(rank < 0, -1, rank + c * (even_kept - KEPT))[:1]
    row = lax.broadcasted_iota(jnp.int32, (KEPT, WIDTH), 0)
    pack = jnp.where(row == goal, 1.0, 0.0).astype(BF)
    lane = lax.broadcasted_iota(jnp.int32, (8, 16), 1)
    from_odd = even_kept + lane
    from_even = jnp.where(KEPT + lane < even_kept, lane, -1)
    slab_goal = jnp.where(lane < 8, jnp.where(c == 0, from_odd, from_even), -1)[:1]
    row = lax.broadcasted_iota(jnp.int32, (KEPT, 16), 0)
    slab_pack = jnp.where(row == slab_goal, 1.0, 0.0).astype(BF)

    stored = []

    def packed(half):
        cols = pl.ds(half * 1024, 1024)
        packed_v[half] = (dot(pack, corr[:, cols]) + dot(slab_pack, slabc[:, cols])).astype(BF)
        for k in range(4):
            there = pruned_o.at[:, pl.ds(half * 1024 + k * 256, 256)]
            copy = pltpu.make_async_copy(packed_v.at[half, :, pl.ds(k * 256, 256)], there, out_s.at[half, k])
            copy.start()
            stored.append(copy)

    for h in range(SPLIT):
        arrived([to_right[h]])
        xtx[h, 0, :32] = (own[h, 1, :32] + xa[h].astype(F32)).astype(BF)
        here, there = xtx.at[h, 0, low], xrx.at[h, 0, low]
        summed.append([send(here, there, e_s.at[h, 2], e_r.at[h, 2], right)])
        arrived([to_left[h]])
        xtx[h, 1, 32:] = (own[h, 3, 32:] + xb[h].astype(F32)).astype(BF)
        here, there = xtx.at[h, 1, top], xrx.at[h, 1, top]
        summed[h].append(send(here, there, e_s.at[h, 3], e_r.at[h, 3], left))
        if h % (SPLIT // 2) == 0:
            packed(h // (SPLIT // 2))

    def z_rows(h, k):
        value = own[h, 0, pl.ds(pl.multiple_of(((z + k) % NZ) * 8, 8), 8)]
        return jnp.concatenate([value[:, : wide // 2], value[:, wide // 2 :]], axis=0)

    zs = {}
    for h in range(SPLIT):
        arrived([pairs[h, 0]])
        total = own[h, 0] + prx[h, 0].astype(F32)
        arrived(plain[h] + summed[h])
        own[h, 0] = total + xrx[h, 0].astype(F32) + xrx[h, 1].astype(F32)
        for k in range(1, NZ):
            ztx[h, k - 1] = z_rows(h, k).astype(BF)
            here, there = ztx.at[h, k - 1], zrx.at[h, k - 1]
            zs[h, k] = send(here, there, w_s.at[h, k - 1], w_r.at[h, k - 1], zdev[k - 1])
    for h in range(SPLIT):
        total = z_rows(h, 0)
        for k in range(1, NZ):
            arrived([zs[h, k]])
            total = total + zrx[h, k - 1].astype(F32)
        mixed_o[:, h * wide : h * wide + wide // 2] = total[:8].astype(BF)
        mixed_o[:, h * wide + wide // 2 : (h + 1) * wide] = total[8:].astype(BF)
    for copy in stored:
        copy.wait()
    for copy in pending:
        copy.wait_send()


def hand_over_kernel(pruned, mixed, pruned_o, mixed_o, pruned_v, mixed_v, in_s, out_s):
    parts = []
    for k in range(PIECES):
        cols = pl.ds(k * (2048 // PIECES), 2048 // PIECES)
        parts.append((pruned.at[:, cols], pruned_v.at[k], pruned_o.at[:, cols]))
    parts.append((mixed, mixed_v, mixed_o))
    arriving = [pltpu.make_async_copy(src, mid, in_s.at[k]) for k, (src, mid, _) in enumerate(parts)]
    leaving = [pltpu.make_async_copy(mid, dst, out_s.at[k]) for k, (_, mid, dst) in enumerate(parts)]
    for copy in arriving:
        copy.start()
    for into, copy in zip(arriving, leaving):
        into.wait()
        copy.start()
    for copy in leaving:
        copy.wait()


def dma(*shape):
    return pltpu.SemaphoreType.DMA(shape)


def vmem():
    return pl.BlockSpec(memory_space=pltpu.VMEM)


def hbm():
    return pl.BlockSpec(memory_space=pl.ANY)


def out(*shape):
    return jax.ShapeDtypeStruct(shape, BF)


def shards(tokens, gate_weight, up_weight, down_weight, inverse_hessian, damping, removed):
    wide = 2048 // SPLIT

    def bf(*shape):
        return pltpu.VMEM(shape, BF)

    def f32(*shape):
        return pltpu.VMEM(shape, F32)

    pruned, mixed = pl.pallas_call(
        prune_kernel,
        out_shape=(out(KEPT, 2048), out(8, 2048)),
        in_specs=[pl.BlockSpec(memory_space=pltpu.SMEM)] + [hbm()] * 7,
        out_specs=(hbm(), vmem()),
        scratch_shapes=[
            bf(8, 2048), bf(WIDTH, 2048), f32(FF // 128, 128), pltpu.VMEM((4, 128), jnp.int32),
            bf(4, BLOCK, FF // 4), bf(2 * WIDTH, 2048),
            bf(2, 2, NX, NZ, 16, 512), bf(2, NX, NZ, 16, 512), bf(2, NZ, NX, 16, 512), bf(2, NX, NZ, 16, 384),
            bf(NY, BLOCK, REM), bf(16, 2048), bf(16, REM),
            bf(2, 16, 1024), bf(2, 16, 384), bf(16, 1024), bf(7, 16, 384), bf(16, 2048), bf(16, REM),
            bf(2, 128, 1024), f32(128, 2 * WIDTH), bf(4, 3, 32, 2 * WIDTH), bf(4, 3, 32, 2 * WIDTH),
            f32(4, 32, 2 * WIDTH), bf(2, 4, 2, 32, WIDTH),
            f32(2 * HALF, HALF), f32(HALF, HALF), f32(WIDTH + 16, REM), bf(WIDTH, 2048), bf(16, 2048),
            bf(SPLIT, 4, 64, wide), bf(SPLIT, 4, 64, wide), f32(SPLIT, 4, 64, wide),
            bf(SPLIT, 64, wide), bf(SPLIT, 32, wide), bf(SPLIT, 32, wide),
            bf(SPLIT, 2, 64, wide), bf(SPLIT, 2, 64, wide),
            bf(SPLIT, 7, 16, wide // 2), bf(SPLIT, 7, 16, wide // 2),
            dma(6), dma(4), dma(1), dma(1), dma(7), dma(7), dma(3), dma(3), dma(5, 7), dma(5, 7),
            dma(4, 4), dma(4, 4), dma(5, 4), dma(5, 4), dma(2), dma(2),
            dma(4, 3), dma(4, 3), dma(4, 3), dma(4, 3),
            dma(SPLIT, 4), dma(SPLIT, 4), dma(SPLIT, 2), dma(SPLIT, 2), dma(SPLIT, 4), dma(SPLIT, 4),
            dma(SPLIT, 7), dma(SPLIT, 7),
            bf(2, KEPT, 1024), dma(2, 4), bf(2048, 2 * WIDTH), dma(3), dma(3),
        ],
        compiler_params=pltpu.CompilerParams(
            collective_id=1, has_side_effects=True, vmem_limit_bytes=VMEM_LIMIT
        ),
        name="prune",
    )(
        removed, tokens, gate_weight.T, up_weight.T, down_weight, inverse_hessian,
        damping.reshape(FF // 128, 128), removed.reshape(4, 128),
    )
    return pl.pallas_call(
        hand_over_kernel,
        out_shape=(out(KEPT, 2048), out(8, 2048)),
        in_specs=[hbm(), hbm()],
        out_specs=(hbm(), hbm()),
        scratch_shapes=[
            bf(PIECES, KEPT, 2048 // PIECES), bf(8, 2048), dma(PIECES + 1), dma(PIECES + 1),
        ],
        compiler_params=pltpu.CompilerParams(vmem_limit_bytes=VMEM_LIMIT),
        name="hand_over",
    )(pruned, mixed)


def solution(mesh):
    in_specs = (
        P("tensor", "dp"),
        P("dp", "tensor"),
        P("dp", "tensor"),
        P("tensor", "dp"),
        P(("tensor", "dp"), None),
        P(),
        P(),
    )
    out_specs = (P("tensor", "dp"), P("tensor", "dp"))
    return jax.shard_map(shards, mesh=mesh, in_specs=in_specs, out_specs=out_specs, check_vma=False)
```

```python
import jax
import jax.numpy as jnp
from jax import lax
from jax.experimental import pallas as pl
from jax.experimental.pallas import tpu as pltpu
from jax.sharding import PartitionSpec as P

MESH = pl.DeviceIdType.MESH
BF = jnp.bfloat16
F32 = jnp.float32
NX, NZ, NY = 4, 8, 4
WIDTH = 416
BLOCK = 104
KEPT = 408
FF = 26624
REM = 512
STEPS = 7
HALF = REM // 2
PIECES = 8
SPLIT = 4
VMEM_LIMIT = 56 * 1024 * 1024


def dot(a, b):
    return jnp.dot(a, b, preferred_element_type=F32)


def place():
    t = lax.axis_index("tensor")
    d = lax.axis_index("dp")
    return t // 16, (t // 2) % 8, t % 2, d


def at(x, z, c, d):
    return (x * 16 + z * 2 + c, d)


def remote(src, dst, send, recv, device):
    return pltpu.make_async_remote_copy(
        src_ref=src, dst_ref=dst, send_sem=send, recv_sem=recv, device_id=device, device_id_type=MESH
    )


def greet(devices):
    barrier = pltpu.get_barrier_semaphore()
    for device in devices:
        pl.semaphore_signal(barrier, inc=1, device_id=device, device_id_type=MESH)
    pl.semaphore_wait(barrier, len(devices))


def pair_indices(removed_s, pair):
    return [removed_s[pair * 16 + j] for j in range(16)]


def index_rows(indices, lanes):
    row = lax.broadcasted_iota(jnp.int32, (16, lanes), 0)
    out = jnp.full((16, lanes), -1, jnp.int32)
    for j, r in enumerate(indices):
        out = jnp.where(row == j, r, out)
    return out


def ranks(indices, first, offset, lanes, rows=16):
    lane = lax.broadcasted_iota(jnp.int32, (rows, lanes), 1) + (first + offset)
    below = jnp.zeros((rows, lanes), jnp.int32)
    gone = jnp.zeros((rows, lanes), jnp.int32)
    for r in indices:
        mine = jnp.where(r >= first, 1, 0)
        below = below + jnp.where(r < lane, mine, 0)
        gone = gone + jnp.where(r == lane, 1, 0)
    return jnp.where(gone > 0, -1, lane - first - below)


def split(value):
    high = value.astype(BF)
    return high, (value - high.astype(F32)).astype(BF)


def dot2(pair, b):
    return dot(pair[0], b) + dot(pair[1], b)


def dot3(a, b):
    return dot(a[0], b[0]) + (dot(a[0], b[1]) + dot(a[1], b[0]))


def newton(xy, between):
    n = HALF
    eye = lax.broadcasted_iota(jnp.int32, (n, n), 0) == lax.broadcasted_iota(jnp.int32, (n, n), 1)
    square = xy[n:, :]
    bound = jnp.max(jnp.sum(jnp.abs(square), axis=0, keepdims=True), axis=1, keepdims=True)
    inverse_bound = 1.0 / bound
    low = 0.9 * inverse_bound
    xy[n:, :] = square * inverse_bound
    for step in range(STEPS):
        middle = 0.5 * (1.0 + low)
        gain = 1.0 / (middle * middle)
        factor = (jnp.where(eye, 2.0 * middle, 0.0) - xy[n:, :]) * gain
        right = split(factor)
        if step == 0:
            xy[n:, :] = dot3(split(xy[n:, :]), right)
            xy[:n, :] = factor * inverse_bound
        elif step < STEPS - 1:
            xy[...] = dot3(split(xy[...]), right)
        else:
            xy[:n, :] = dot3(split(xy[:n, :]), right)
        low = low * gain
        between(step)
    xy[:n, :] = xy[:n, :] * (2.0 / (1.0 + low))


def prune_kernel(
    removed_s, tok_h, gate_h, up_h, down_h, hess_h, damp_h, removed_h,
    pruned_o, mixed_o,
    tok_in, down, damp, removed_v, hbuf, weight,
    tok_o, l_a, l_b, s_o, hkr_o, slabd_o, slabh_o,
    lpad, spad, l_rx, s_rx, slabd_tx, slabh_tx,
    lhs, pre, pre_tx, pre_rx, pre_own, hid,
    xy, inv, rows, corr, slabc,
    ptx, prx, own, x2, xa, xb, xtx, xrx, ztx, zrx,
    load_s, hess_s, pair_s, pair_r, sc_s, sc_r, y_s, y_r, z_s, z_r, x_s, x_r, c_s, c_r, sl_s, sl_r,
    ps_s, ps_r, h_s, h_r,
    p_s, p_r, a_s, a_r, e_s, e_r, w_s, w_r, packed_v, out_s, turned, lx_s, lx_r,
):
    x, z, c, d = place()
    other = 1 - c
    pair = x * NZ + z
    first = (pair * 2 + c) * WIDTH
    quarter = FF // 4

    def load(src, dst, sem):
        copy = pltpu.make_async_copy(src, dst, sem)
        copy.start()
        return copy

    tok_load = load(tok_h, tok_in, load_s.at[0])
    removed_load = load(removed_h, removed_v, load_s.at[1])
    damp_load = load(damp_h, damp, load_s.at[2])
    hess_loads = [load(hess_h.at[:, pl.ds(g * quarter, quarter)], hbuf.at[g], hess_s.at[g]) for g in range(4)]
    down_load = load(down_h, down, load_s.at[3])
    gate_load = load(gate_h, weight.at[pl.ds(0, WIDTH)], load_s.at[4])
    up_load = load(up_h, weight.at[pl.ds(WIDTH, WIDTH)], load_s.at[5])

    partner = at(x, z, other, d)
    right, left = at((x + 1) % NX, z, c, d), at((x + 3) % NX, z, c, d)
    ydev = [at(x, z, c, (d + k) % NY) for k in range(1, NY)]
    ycross = [at(x, z, other, (d + k) % NY) for k in range(1, NY)]
    across = at((x + 2) % NX, z, c, d)
    zdev = [at(x, (z + k) % NZ, c, d) for k in range(1, NZ)]
    greet([partner, right, left, across] + ydev + ycross + zdev)
    pending = []

    def send(src, dst, s, r, device):
        copy = remote(src, dst, s, r, device)
        copy.start()
        pending.append(copy)
        return copy

    def arrived(copies):
        for copy in copies:
            copy.wait_recv()

    def z_sends(array, n):
        here = array.at[c, x, z]
        return [send(here, here, z_s.at[n, k], z_r.at[n, k], zdev[k]) for k in range(NZ - 1)]

    def x_sends(array, n):
        here = array.at[c, x]
        return [
            send(here, here, x_s.at[n, 0], x_r.at[n, 0], right),
            send(here, here, x_s.at[n, 1], x_r.at[n, 1], left),
        ]

    def x_forwards(array, n):
        low = array.at[c, (x + 3) % NX, pl.ds(0, 4)]
        high = array.at[c, (x + 1) % NX, pl.ds(4, 4)]
        return [
            send(low, low, x_s.at[n, 2], x_r.at[n, 2], right),
            send(high, high, x_s.at[n, 3], x_r.at[n, 3], left),
        ]

    def core_send(array, n, k):
        here = array.at[c, (x + k) % NX]
        return send(here, here, c_s.at[n, k], c_r.at[n, k], partner)

    tok_load.wait()
    tok = tok_in[...].astype(F32)
    for h in range(2):
        cols = slice(h * 512, h * 512 + 512)
        tok_o[h, c, x, z] = jnp.concatenate([tok[:, :1024][:, cols], tok[:, 1024:][:, cols]], axis=0).astype(BF)
    tok_z = [z_sends(tok_o.at[h], 2 * h) for h in range(2)]

    indices = pair_indices(removed_s, pair)
    removed_load.wait()
    chunk = quarter // 4
    lane = lax.broadcasted_iota(jnp.int32, (1, 128), 1)
    channel = lax.broadcasted_iota(jnp.int32, (chunk, 128), 0)
    for g in range(4):
        hess_loads[g].wait()
        wanted = removed_v[g : g + 1, :] - (g * quarter + (lane // 32) * chunk)
        hot = jnp.where(channel == wanted, 1.0, 0.0).astype(BF)
        total = jnp.zeros((BLOCK, 128), F32)
        for q in range(4):
            part = dot(hbuf[g, :, q * chunk : (q + 1) * chunk], hot)
            total = jnp.where(lane // 32 == q, part, total)
        hkr_o[d, :, g * 128 : (g + 1) * 128] = total.astype(BF)
    rows104 = index_rows(indices, BLOCK)
    lane104 = lax.broadcasted_iota(jnp.int32, (16, BLOCK), 1)
    block_first = first + d * BLOCK
    pick104 = jnp.where(lane104 + block_first == rows104, 1.0, 0.0)
    own_rows = dot(pick104.astype(BF), hkr_o[d]).astype(BF)
    damp_load.wait()
    lane128 = lax.broadcasted_iota(jnp.int32, (16, 128), 1)
    row128 = lax.broadcasted_iota(jnp.int32, (16, 128), 0)
    found = jnp.zeros((16, 128), F32)
    for j, r in enumerate(indices):
        line = damp[pl.ds(r // 128, 1), :]
        here = jnp.where(r >= block_first, jnp.where(r < block_first + BLOCK, j, -1), -1)
        found = jnp.where(row128 == here, jnp.where(lane128 == r % 128, line, 0.0), found)
    damped = jnp.sum(found, axis=1, keepdims=True)
    high = damped.astype(BF).astype(F32)
    extra = jnp.where(lane128 == 0, high, jnp.where(lane128 == 1, damped - high, 0.0)).astype(BF)
    for half in range(2):
        spad[half, :, :256] = own_rows[:, half * 256 : (half + 1) * 256]
        spad[half, :, 256:] = extra
    s_sends = []
    for k in range(NY - 1):
        s_sends.append(send(spad.at[c], s_rx.at[k], sc_s.at[k], sc_r.at[k], ydev[k]))
        s_sends.append(send(spad.at[other], s_rx.at[3 + k], sc_s.at[3 + k], sc_r.at[3 + k], ycross[k]))
    s_sends.append(send(spad.at[other], s_rx.at[6], sc_s.at[6], sc_r.at[6], partner))
    h_sends = [send(hkr_o.at[d], hkr_o.at[d], y_s.at[k], y_r.at[k], ydev[k]) for k in range(NY - 1)]

    down_load.wait()
    rows416 = index_rows(indices, WIDTH)
    lane416 = lax.broadcasted_iota(jnp.int32, (16, WIDTH), 1)
    pick = jnp.where(lane416 + first == rows416, 1.0, 0.0).astype(BF)
    lost = dot(pick, down[...]).astype(BF)
    lpad[0] = lost[:, :1024]
    lpad[1] = lost[:, 1024:]
    l_pair = send(lpad.at[other], l_rx, pair_s.at[0], pair_r.at[0], partner)
    row16 = lax.broadcasted_iota(jnp.int32, (16, WIDTH), 0)
    target = jnp.where(row16 < 8, row16 + (1 - c) * KEPT, -7)
    slab_pick = jnp.where(ranks(indices, first, 0, WIDTH) == target, 1.0, 0.0)
    slabd_tx[...] = dot(slab_pick.astype(BF), down[...]).astype(BF)
    slabd = send(slabd_tx, slabd_o, sl_s.at[0], sl_r.at[0], partner)

    gate_load.wait()
    up_load.wait()
    for i in range(4):
        turned[512 * i : 512 * i + 512] = weight[:, 512 * i : 512 * i + 512].T
    arrived(s_sends)
    total = spad[c].astype(F32)
    for k in range(7):
        total = total + s_rx[k].astype(F32)
    s_o[c, x, z] = total.astype(BF)
    s_z = z_sends(s_o, 3)
    arrived([l_pair])
    value = lpad[c] + l_rx[...]
    l_a[c, x, z] = value[:, :512]
    l_b[c, z, x] = value[:, 512:]
    here = l_b.at[c, z, x]
    lb_x = [send(here, here, lx_s.at[k], lx_r.at[k], (right, across, left)[k]) for k in range(3)]
    tok_x = []
    for h in range(2):
        arrived(tok_z[h])
        tok_x.append(x_sends(tok_o.at[h], 2 * h))
    tok_c = {0: [core_send(tok_o.at[h], 2 * h, 0) for h in range(2)]}
    l_z = z_sends(l_a, 1)
    arrived(lb_x)
    here = l_b.at[c, z]
    lb_z = [send(here, here, z_s.at[4, k], z_r.at[4, k], zdev[k]) for k in range(NZ - 1)]
    arrived(s_z)
    s_x = x_sends(s_o, 3)
    s_c = [core_send(s_o, 3, 0)]

    partials = {}

    def preact(k):
        arrived(tok_c[k])
        b = (x + k) % NX
        for core in range(2):
            for h in range(2):
                value = tok_o[h, core, b].astype(F32)
                cols = slice(h * 512, h * 512 + 512)
                lhs[0, core * 64 : core * 64 + 64, cols] = value[:, :8].reshape(64, 512).astype(BF)
                lhs[1, core * 64 : core * 64 + 64, cols] = value[:, 8:].reshape(64, 512).astype(BF)
        pre[...] = dot(lhs[0], turned[:1024]) + dot(lhs[1], turned[1024:])
        sends = []
        for m in range(NY - 1):
            part = pl.ds(pl.multiple_of(((d + 1 + m) % NY) * 32, 32), 32)
            pre_tx[k, m] = pre[part, :].astype(BF)
            sends.append(send(pre_tx.at[k, m], pre_rx.at[k, m], ps_s.at[k, m], ps_r.at[k, m], ydev[m]))
        pre_own[k] = pre[pl.ds(pl.multiple_of(d * 32, 32), 32), :]
        partials[k] = sends

    shares = {}

    def gated(k):
        arrived(partials[k])
        value = pre_own[k]
        for m in range(NY - 1):
            value = value + pre_rx[k, m].astype(F32)
        gate, up = value[:, :WIDTH], value[:, WIDTH:]
        lane = lax.broadcasted_iota(jnp.int32, (32, WIDTH), 1) + first
        hidden = gate / (1.0 + jnp.exp(-gate)) * up
        for r in indices:
            hidden = jnp.where(lane == r, 0.0, hidden)
        hid[d // 2, k, d % 2] = hidden.astype(BF)
        here = hid.at[d // 2, k, d % 2]
        shares[k] = [send(here, here, h_s.at[k, m], h_r.at[k, m], ydev[m]) for m in range(NY - 1)]

    preact(0)
    tok_f = []
    tok_c[1], tok_c[3] = [], []
    for h in range(2):
        arrived(tok_x[h])
        tok_f.append(x_forwards(tok_o.at[h], 2 * h))
        tok_c[1].append(core_send(tok_o.at[h], 2 * h, 1))
        tok_c[3].append(core_send(tok_o.at[h], 2 * h, 3))
    arrived(s_x)
    s_f = x_forwards(s_o, 3)
    s_c += [core_send(s_o, 3, 1), core_send(s_o, 3, 3)]
    preact(1)
    arrived(s_f)
    s_c.append(core_send(s_o, 3, 2))
    preact(3)
    arrived(l_z)
    later = {"x": x_sends(l_a, 1), "c": [core_send(l_a, 1, 0)]}

    def tokens_last():
        tok_c[2] = []
        for h in range(2):
            arrived(tok_f[h])
            tok_c[2].append(core_send(tok_o.at[h], 2 * h, 2))

    def lost_forward():
        arrived(later["x"])
        later["f"] = x_forwards(l_a, 1)
        later["c"] += [core_send(l_a, 1, 1), core_send(l_a, 1, 3)]

    def lost_other():
        arrived(lb_z)
        later["c"].append(send(l_b.at[c], l_b.at[c], c_s.at[4, 0], c_r.at[4, 0], partner))

    def lost_last():
        arrived(later["f"])
        later["c"].append(core_send(l_a, 1, 2))

    def gather_rows():
        arrived(h_sends)
        slab = jnp.zeros((16, REM), F32)
        for k in range(NY):
            mine = ranks(indices, first, k * BLOCK, BLOCK) == target[:, :BLOCK]
            slab = slab + dot(jnp.where(mine, 1.0, 0.0).astype(BF), hkr_o[k])
            rows[k * BLOCK : (k + 1) * BLOCK] = hkr_o[k].astype(F32)
        slabh_tx[...] = slab.astype(BF)
        later["s"] = send(slabh_tx, slabh_o, sl_s.at[1], sl_r.at[1], partner)

    eye = lax.broadcasted_iota(jnp.int32, (HALF, HALF), 0) == lax.broadcasted_iota(jnp.int32, (HALF, HALF), 1)

    def s_block(i, j):
        return s_o[j, 2 * i : 2 * i + 2, :, :, :256].reshape(HALF, 256)

    def diagonal(i):
        damping = s_o[0, 2 * i : 2 * i + 2, :, :, 256:].reshape(HALF, 128).astype(F32)
        return jnp.where(eye, damping[:, 0:1] + damping[:, 1:2], 0.0)

    tokens_last()
    arrived(s_c)
    xy[HALF:, :] = s_block(0, 0).astype(F32) + diagonal(0)
    tasks = {1: [lambda: preact(2)], 4: [lambda: gated(0)], 6: [lost_forward, lambda: gated(1)]}
    more_tasks = {
        0: [lambda: gated(3)], 2: [lost_other], 3: [lambda: gated(2)], 5: [lost_last],
    }

    def between(plan):
        def run(step):
            for task in plan.get(step, []):
                task()

        return run

    newton(xy, between(tasks))
    gather_rows()
    inv[...] = xy[:HALF, :]
    a_inv = split(inv[...])
    b_block = s_block(0, 1)
    v = dot(s_block(1, 0), a_inv[0]) + dot(s_block(1, 0), a_inv[1])
    xy[HALF:, :] = s_block(1, 1).astype(F32) + diagonal(1) - dot2(split(v), b_block)
    newton(xy, between(more_tasks))
    e_inv = split(xy[:HALF, :])
    arrived([slabd, later["s"]])
    rows[WIDTH:] = slabh_o[...].astype(F32)
    q = dot(rows[:, :HALF].astype(BF), a_inv[0]) + dot(rows[:, :HALF].astype(BF), a_inv[1])
    u = rows[:, HALF:] - dot2(split(q), b_block)
    second = dot3(split(u), e_inv)
    coef = [(q - dot3(split(second), split(v))).astype(BF), second.astype(BF)]
    arrived(later["c"])
    for half in range(2):
        first_rows = l_a[half].reshape(REM, 512)
        other_rows = jnp.concatenate([l_b[half, :, k].reshape(128, 512) for k in range(NX)], axis=0)
        for piece, lost_rows in enumerate((first_rows, other_rows)):
            cols = pl.ds(half * 1024 + piece * 512, 512)
            change = dot(coef[0], lost_rows[:HALF]) + dot(coef[1], lost_rows[HALF:])
            corr[:, cols] = (down[:, cols].astype(F32) - change[:WIDTH]).astype(BF)
            slabc[:, cols] = (slabd_o[:, cols].astype(F32) - change[WIDTH:]).astype(BF)

    wide = 2048 // SPLIT
    scale = FF ** (-0.5)
    order = (2, 1, 3, 0)
    low, top = pl.ds(0, 32), pl.ds(32, 32)
    pairs, to_right, to_left, plain, summed = {}, [], [], [], []
    for k in order:
        arrived(shares[k])

    def product(core, h):
        cols = pl.ds(h * wide, wide)
        return dot(hid[core].reshape(256, WIDTH), corr[:, cols]) * scale

    for h in range(SPLIT):
        ptx[h] = product(other, h).reshape(4, 64, wide).astype(BF)
        for k in order:
            pairs[h, k] = send(ptx.at[h, k], prx.at[h, k], p_s.at[h, k], p_r.at[h, k], partner)
    for h in range(SPLIT):
        own[h] = product(c, h).reshape(4, 64, wide)
        arrived([pairs[h, 2]])
        x2[h] = (own[h, 2] + prx[h, 2].astype(F32)).astype(BF)
        to_right.append(send(x2.at[h, low], xa.at[h], a_s.at[h, 0], a_r.at[h, 0], right))
        to_left.append(send(x2.at[h, top], xb.at[h], a_s.at[h, 1], a_r.at[h, 1], left))
        arrived([pairs[h, 1]])
        own[h, 1] = own[h, 1] + prx[h, 1].astype(F32)
        xtx[h, 0, 32:] = own[h, 1, 32:].astype(BF)
        here, there = xtx.at[h, 0, top], xrx.at[h, 0, top]
        plain.append([send(here, there, e_s.at[h, 0], e_r.at[h, 0], right)])
        arrived([pairs[h, 3]])
        own[h, 3] = own[h, 3] + prx[h, 3].astype(F32)
        xtx[h, 1, :32] = own[h, 3, :32].astype(BF)
        here, there = xtx.at[h, 1, low], xrx.at[h, 1, low]
        plain[h].append(send(here, there, e_s.at[h, 1], e_r.at[h, 1], left))

    even = (pair * 2 + 1) * WIDTH
    even_kept = WIDTH
    for r in indices:
        even_kept = even_kept - jnp.where(r < even, 1, 0)
    rank = ranks(indices, first, 0, WIDTH, 8)
    goal = jnp.where(rank < 0, -1, rank + c * (even_kept - KEPT))[:1]
    row = lax.broadcasted_iota(jnp.int32, (KEPT, WIDTH), 0)
    pack = jnp.where(row == goal, 1.0, 0.0).astype(BF)
    lane = lax.broadcasted_iota(jnp.int32, (8, 16), 1)
    from_odd = even_kept + lane
    from_even = jnp.where(KEPT + lane < even_kept, lane, -1)
    slab_goal = jnp.where(lane < 8, jnp.where(c == 0, from_odd, from_even), -1)[:1]
    row = lax.broadcasted_iota(jnp.int32, (KEPT, 16), 0)
    slab_pack = jnp.where(row == slab_goal, 1.0, 0.0).astype(BF)

    stored = []

    def packed(half):
        cols = pl.ds(half * 1024, 1024)
        packed_v[half] = (dot(pack, corr[:, cols]) + dot(slab_pack, slabc[:, cols])).astype(BF)
        for k in range(4):
            there = pruned_o.at[:, pl.ds(half * 1024 + k * 256, 256)]
            copy = pltpu.make_async_copy(packed_v.at[half, :, pl.ds(k * 256, 256)], there, out_s.at[half, k])
            copy.start()
            stored.append(copy)

    for h in range(SPLIT):
        arrived([to_right[h]])
        xtx[h, 0, :32] = (own[h, 1, :32] + xa[h].astype(F32)).astype(BF)
        here, there = xtx.at[h, 0, low], xrx.at[h, 0, low]
        summed.append([send(here, there, e_s.at[h, 2], e_r.at[h, 2], right)])
        arrived([to_left[h]])
        xtx[h, 1, 32:] = (own[h, 3, 32:] + xb[h].astype(F32)).astype(BF)
        here, there = xtx.at[h, 1, top], xrx.at[h, 1, top]
        summed[h].append(send(here, there, e_s.at[h, 3], e_r.at[h, 3], left))
        if h % (SPLIT // 2) == 0:
            packed(h // (SPLIT // 2))

    def z_rows(h, k):
        value = own[h, 0, pl.ds(pl.multiple_of(((z + k) % NZ) * 8, 8), 8)]
        return jnp.concatenate([value[:, : wide // 2], value[:, wide // 2 :]], axis=0)

    zs = {}
    for h in range(SPLIT):
        arrived([pairs[h, 0]])
        total = own[h, 0] + prx[h, 0].astype(F32)
        arrived(plain[h] + summed[h])
        own[h, 0] = total + xrx[h, 0].astype(F32) + xrx[h, 1].astype(F32)
        for k in range(1, NZ):
            ztx[h, k - 1] = z_rows(h, k).astype(BF)
            here, there = ztx.at[h, k - 1], zrx.at[h, k - 1]
            zs[h, k] = send(here, there, w_s.at[h, k - 1], w_r.at[h, k - 1], zdev[k - 1])
    for h in range(SPLIT):
        total = z_rows(h, 0)
        for k in range(1, NZ):
            arrived([zs[h, k]])
            total = total + zrx[h, k - 1].astype(F32)
        mixed_o[:, h * wide : h * wide + wide // 2] = total[:8].astype(BF)
        mixed_o[:, h * wide + wide // 2 : (h + 1) * wide] = total[8:].astype(BF)
    for copy in stored:
        copy.wait()
    for copy in pending:
        copy.wait_send()


def hand_over_kernel(pruned, mixed, pruned_o, mixed_o, pruned_v, mixed_v, in_s, out_s):
    parts = []
    for k in range(PIECES):
        cols = pl.ds(k * (2048 // PIECES), 2048 // PIECES)
        parts.append((pruned.at[:, cols], pruned_v.at[k], pruned_o.at[:, cols]))
    parts.append((mixed, mixed_v, mixed_o))
    arriving = [pltpu.make_async_copy(src, mid, in_s.at[k]) for k, (src, mid, _) in enumerate(parts)]
    leaving = [pltpu.make_async_copy(mid, dst, out_s.at[k]) for k, (_, mid, dst) in enumerate(parts)]
    for copy in arriving:
        copy.start()
    for into, copy in zip(arriving, leaving):
        into.wait()
        copy.start()
    for copy in leaving:
        copy.wait()


def dma(*shape):
    return pltpu.SemaphoreType.DMA(shape)


def vmem():
    return pl.BlockSpec(memory_space=pltpu.VMEM)


def hbm():
    return pl.BlockSpec(memory_space=pl.ANY)


def out(*shape):
    return jax.ShapeDtypeStruct(shape, BF)


def shards(tokens, gate_weight, up_weight, down_weight, inverse_hessian, damping, removed):
    wide = 2048 // SPLIT

    def bf(*shape):
        return pltpu.VMEM(shape, BF)

    def f32(*shape):
        return pltpu.VMEM(shape, F32)

    pruned, mixed = pl.pallas_call(
        prune_kernel,
        out_shape=(out(KEPT, 2048), out(8, 2048)),
        in_specs=[pl.BlockSpec(memory_space=pltpu.SMEM)] + [hbm()] * 7,
        out_specs=(hbm(), vmem()),
        scratch_shapes=[
            bf(8, 2048), bf(WIDTH, 2048), f32(FF // 128, 128), pltpu.VMEM((4, 128), jnp.int32),
            bf(4, BLOCK, FF // 4), bf(2 * WIDTH, 2048),
            bf(2, 2, NX, NZ, 16, 512), bf(2, NX, NZ, 16, 512), bf(2, NZ, NX, 16, 512), bf(2, NX, NZ, 16, 384),
            bf(NY, BLOCK, REM), bf(16, 2048), bf(16, REM),
            bf(2, 16, 1024), bf(2, 16, 384), bf(16, 1024), bf(7, 16, 384), bf(16, 2048), bf(16, REM),
            bf(2, 128, 1024), f32(128, 2 * WIDTH), bf(4, 3, 32, 2 * WIDTH), bf(4, 3, 32, 2 * WIDTH),
            f32(4, 32, 2 * WIDTH), bf(2, 4, 2, 32, WIDTH),
            f32(2 * HALF, HALF), f32(HALF, HALF), f32(WIDTH + 16, REM), bf(WIDTH, 2048), bf(16, 2048),
            bf(SPLIT, 4, 64, wide), bf(SPLIT, 4, 64, wide), f32(SPLIT, 4, 64, wide),
            bf(SPLIT, 64, wide), bf(SPLIT, 32, wide), bf(SPLIT, 32, wide),
            bf(SPLIT, 2, 64, wide), bf(SPLIT, 2, 64, wide),
            bf(SPLIT, 7, 16, wide // 2), bf(SPLIT, 7, 16, wide // 2),
            dma(6), dma(4), dma(1), dma(1), dma(7), dma(7), dma(3), dma(3), dma(5, 7), dma(5, 7),
            dma(4, 4), dma(4, 4), dma(5, 4), dma(5, 4), dma(2), dma(2),
            dma(4, 3), dma(4, 3), dma(4, 3), dma(4, 3),
            dma(SPLIT, 4), dma(SPLIT, 4), dma(SPLIT, 2), dma(SPLIT, 2), dma(SPLIT, 4), dma(SPLIT, 4),
            dma(SPLIT, 7), dma(SPLIT, 7),
            bf(2, KEPT, 1024), dma(2, 4), bf(2048, 2 * WIDTH), dma(3), dma(3),
        ],
        compiler_params=pltpu.CompilerParams(
            collective_id=1, has_side_effects=True, vmem_limit_bytes=VMEM_LIMIT
        ),
        name="prune",
    )(
        removed, tokens, gate_weight.T, up_weight.T, down_weight, inverse_hessian,
        damping.reshape(FF // 128, 128), removed.reshape(4, 128),
    )
    return pl.pallas_call(
        hand_over_kernel,
        out_shape=(out(KEPT, 2048), out(8, 2048)),
        in_specs=[hbm(), hbm()],
        out_specs=(hbm(), hbm()),
        scratch_shapes=[
            bf(PIECES, KEPT, 2048 // PIECES), bf(8, 2048), dma(PIECES + 1), dma(PIECES + 1),
        ],
        compiler_params=pltpu.CompilerParams(vmem_limit_bytes=VMEM_LIMIT),
        name="hand_over",
    )(pruned, mixed)


def solution(mesh):
    in_specs = (
        P("tensor", "dp"),
        P("dp", "tensor"),
        P("dp", "tensor"),
        P("tensor", "dp"),
        P(("tensor", "dp"), None),
        P(),
        P(),
    )
    out_specs = (P("tensor", "dp"), P("tensor", "dp"))
    return jax.shard_map(shards, mesh=mesh, in_specs=in_specs, out_specs=out_specs, check_vma=False)
```

```python
import jax
import jax.numpy as jnp
from jax import lax
from jax.experimental import pallas as pl
from jax.experimental.pallas import tpu as pltpu
from jax.sharding import PartitionSpec as P

MESH = pl.DeviceIdType.MESH
BF = jnp.bfloat16
F32 = jnp.float32
NX, NZ, NY = 4, 8, 4
WIDTH = 416
BLOCK = 104
KEPT = 408
FF = 26624
REM = 512
STEPS = 7
HALF = REM // 2
PIECES = 8
SPLIT = 4
VMEM_LIMIT = 56 * 1024 * 1024


def dot(a, b):
    return jnp.dot(a, b, preferred_element_type=F32)


def place():
    t = lax.axis_index("tensor")
    d = lax.axis_index("dp")
    return t // 16, (t // 2) % 8, t % 2, d


def at(x, z, c, d):
    return (x * 16 + z * 2 + c, d)


def remote(src, dst, send, recv, device):
    return pltpu.make_async_remote_copy(
        src_ref=src, dst_ref=dst, send_sem=send, recv_sem=recv, device_id=device, device_id_type=MESH
    )


def greet(devices):
    barrier = pltpu.get_barrier_semaphore()
    for device in devices:
        pl.semaphore_signal(barrier, inc=1, device_id=device, device_id_type=MESH)
    pl.semaphore_wait(barrier, len(devices))


def pair_indices(removed_s, pair):
    return [removed_s[pair * 16 + j] for j in range(16)]


def index_rows(indices, lanes):
    row = lax.broadcasted_iota(jnp.int32, (16, lanes), 0)
    out = jnp.full((16, lanes), -1, jnp.int32)
    for j, r in enumerate(indices):
        out = jnp.where(row == j, r, out)
    return out


def ranks(indices, first, offset, lanes, rows=16):
    lane = lax.broadcasted_iota(jnp.int32, (rows, lanes), 1) + (first + offset)
    below = jnp.zeros((rows, lanes), jnp.int32)
    gone = jnp.zeros((rows, lanes), jnp.int32)
    for r in indices:
        mine = jnp.where(r >= first, 1, 0)
        below = below + jnp.where(r < lane, mine, 0)
        gone = gone + jnp.where(r == lane, 1, 0)
    return jnp.where(gone > 0, -1, lane - first - below)


def split(value):
    high = value.astype(BF)
    return high, (value - high.astype(F32)).astype(BF)


def dot2(pair, b):
    return dot(pair[0], b) + dot(pair[1], b)


def dot3(a, b):
    return dot(a[0], b[0]) + (dot(a[0], b[1]) + dot(a[1], b[0]))


def newton(xy, between):
    n = HALF
    eye = lax.broadcasted_iota(jnp.int32, (n, n), 0) == lax.broadcasted_iota(jnp.int32, (n, n), 1)
    square = xy[n:, :]
    bound = jnp.max(jnp.sum(jnp.abs(square), axis=0, keepdims=True), axis=1, keepdims=True)
    inverse_bound = 1.0 / bound
    low = 0.9 * inverse_bound
    xy[n:, :] = square * inverse_bound
    for step in range(STEPS):
        middle = 0.5 * (1.0 + low)
        gain = 1.0 / (middle * middle)
        factor = (jnp.where(eye, 2.0 * middle, 0.0) - xy[n:, :]) * gain
        right = split(factor)
        if step == 0:
            xy[n:, :] = dot3(split(xy[n:, :]), right)
            xy[:n, :] = factor * inverse_bound
        elif step < STEPS - 1:
            xy[...] = dot3(split(xy[...]), right)
        else:
            xy[:n, :] = dot3(split(xy[:n, :]), right)
        low = low * gain
        between(step)
    xy[:n, :] = xy[:n, :] * (2.0 / (1.0 + low))


def prune_kernel(
    removed_s, tok_h, gate_h, up_h, down_h, hess_h, damp_h, removed_h,
    pruned_o, mixed_o,
    tok_in, down, damp, removed_v, hbuf, weight,
    tok_o, l_a, l_b, s_o, hkr_o, slabd_o, slabh_o,
    lpad, spad, l_rx, s_rx, slabd_tx, slabh_tx,
    lhs, pre, pre_tx, pre_rx, pre_own, hid,
    xy, inv, rows, corr, slabc,
    ptx, prx, own, x2, xa, xb, xtx, xrx, ztx, zrx,
    load_s, hess_s, pair_s, pair_r, sc_s, sc_r, y_s, y_r, z_s, z_r, x_s, x_r, c_s, c_r, sl_s, sl_r,
    ps_s, ps_r, h_s, h_r,
    p_s, p_r, a_s, a_r, e_s, e_r, w_s, w_r, packed_v, out_s, turned, lx_s, lx_r,
):
    x, z, c, d = place()
    other = 1 - c
    pair = x * NZ + z
    first = (pair * 2 + c) * WIDTH
    quarter = FF // 4

    def load(src, dst, sem):
        copy = pltpu.make_async_copy(src, dst, sem)
        copy.start()
        return copy

    tok_load = load(tok_h, tok_in, load_s.at[0])
    removed_load = load(removed_h, removed_v, load_s.at[1])
    damp_load = load(damp_h, damp, load_s.at[2])
    hess_loads = [load(hess_h.at[:, pl.ds(g * quarter, quarter)], hbuf.at[g], hess_s.at[g]) for g in range(4)]
    down_load = load(down_h, down, load_s.at[3])
    gate_load = load(gate_h, weight.at[pl.ds(0, WIDTH)], load_s.at[4])
    up_load = load(up_h, weight.at[pl.ds(WIDTH, WIDTH)], load_s.at[5])

    partner = at(x, z, other, d)
    right, left = at((x + 1) % NX, z, c, d), at((x + 3) % NX, z, c, d)
    ydev = [at(x, z, c, (d + k) % NY) for k in range(1, NY)]
    ycross = [at(x, z, other, (d + k) % NY) for k in range(1, NY)]
    across = at((x + 2) % NX, z, c, d)
    zdev = [at(x, (z + k) % NZ, c, d) for k in range(1, NZ)]
    greet([partner, right, left, across] + ydev + ycross + zdev)
    pending = []

    def send(src, dst, s, r, device):
        copy = remote(src, dst, s, r, device)
        copy.start()
        pending.append(copy)
        return copy

    def arrived(copies):
        for copy in copies:
            copy.wait_recv()

    def z_sends(array, n):
        here = array.at[c, x, z]
        return [send(here, here, z_s.at[n, k], z_r.at[n, k], zdev[k]) for k in range(NZ - 1)]

    def x_sends(array, n):
        here = array.at[c, x]
        return [
            send(here, here, x_s.at[n, 0], x_r.at[n, 0], right),
            send(here, here, x_s.at[n, 1], x_r.at[n, 1], left),
        ]

    def x_forwards(array, n):
        low = array.at[c, (x + 3) % NX, pl.ds(0, 4)]
        high = array.at[c, (x + 1) % NX, pl.ds(4, 4)]
        return [
            send(low, low, x_s.at[n, 2], x_r.at[n, 2], right),
            send(high, high, x_s.at[n, 3], x_r.at[n, 3], left),
        ]

    def core_send(array, n, k):
        here = array.at[c, (x + k) % NX]
        return send(here, here, c_s.at[n, k], c_r.at[n, k], partner)

    tok_load.wait()
    tok = tok_in[...].astype(F32)
    for h in range(2):
        cols = slice(h * 512, h * 512 + 512)
        tok_o[h, c, x, z] = jnp.concatenate([tok[:, :1024][:, cols], tok[:, 1024:][:, cols]], axis=0).astype(BF)
    tok_z = [z_sends(tok_o.at[h], 2 * h) for h in range(2)]

    indices = pair_indices(removed_s, pair)
    removed_load.wait()
    chunk = quarter // 4
    lane = lax.broadcasted_iota(jnp.int32, (1, 128), 1)
    channel = lax.broadcasted_iota(jnp.int32, (chunk, 128), 0)
    for g in range(4):
        hess_loads[g].wait()
        wanted = removed_v[g : g + 1, :] - (g * quarter + (lane // 32) * chunk)
        hot = jnp.where(channel == wanted, 1.0, 0.0).astype(BF)
        total = jnp.zeros((BLOCK, 128), F32)
        for q in range(4):
            part = dot(hbuf[g, :, q * chunk : (q + 1) * chunk], hot)
            total = jnp.where(lane // 32 == q, part, total)
        hkr_o[d, :, g * 128 : (g + 1) * 128] = total.astype(BF)
    rows104 = index_rows(indices, BLOCK)
    lane104 = lax.broadcasted_iota(jnp.int32, (16, BLOCK), 1)
    block_first = first + d * BLOCK
    pick104 = jnp.where(lane104 + block_first == rows104, 1.0, 0.0)
    own_rows = dot(pick104.astype(BF), hkr_o[d]).astype(BF)
    damp_load.wait()
    lane128 = lax.broadcasted_iota(jnp.int32, (16, 128), 1)
    row128 = lax.broadcasted_iota(jnp.int32, (16, 128), 0)
    found = jnp.zeros((16, 128), F32)
    for j, r in enumerate(indices):
        line = damp[pl.ds(r // 128, 1), :]
        here = jnp.where(r >= block_first, jnp.where(r < block_first + BLOCK, j, -1), -1)
        found = jnp.where(row128 == here, jnp.where(lane128 == r % 128, line, 0.0), found)
    damped = jnp.sum(found, axis=1, keepdims=True)
    high = damped.astype(BF).astype(F32)
    extra = jnp.where(lane128 == 0, high, jnp.where(lane128 == 1, damped - high, 0.0)).astype(BF)
    for half in range(2):
        spad[half, :, :256] = own_rows[:, half * 256 : (half + 1) * 256]
        spad[half, :, 256:] = extra
    s_sends = []
    for k in range(NY - 1):
        s_sends.append(send(spad.at[c], s_rx.at[k], sc_s.at[k], sc_r.at[k], ydev[k]))
        s_sends.append(send(spad.at[other], s_rx.at[3 + k], sc_s.at[3 + k], sc_r.at[3 + k], ycross[k]))
    s_sends.append(send(spad.at[other], s_rx.at[6], sc_s.at[6], sc_r.at[6], partner))
    h_sends = [send(hkr_o.at[d], hkr_o.at[d], y_s.at[k], y_r.at[k], ydev[k]) for k in range(NY - 1)]

    down_load.wait()
    rows416 = index_rows(indices, WIDTH)
    lane416 = lax.broadcasted_iota(jnp.int32, (16, WIDTH), 1)
    pick = jnp.where(lane416 + first == rows416, 1.0, 0.0).astype(BF)
    lost = dot(pick, down[...]).astype(BF)
    lpad[0] = lost[:, :1024]
    lpad[1] = lost[:, 1024:]
    l_pair = send(lpad.at[other], l_rx, pair_s.at[0], pair_r.at[0], partner)
    row16 = lax.broadcasted_iota(jnp.int32, (16, WIDTH), 0)
    target = jnp.where(row16 < 8, row16 + (1 - c) * KEPT, -7)
    slab_pick = jnp.where(ranks(indices, first, 0, WIDTH) == target, 1.0, 0.0)
    slabd_tx[...] = dot(slab_pick.astype(BF), down[...]).astype(BF)
    slabd = send(slabd_tx, slabd_o, sl_s.at[0], sl_r.at[0], partner)

    gate_load.wait()
    up_load.wait()
    for i in range(4):
        turned[512 * i : 512 * i + 512] = weight[:, 512 * i : 512 * i + 512].T
    arrived(s_sends)
    total = spad[c].astype(F32)
    for k in range(7):
        total = total + s_rx[k].astype(F32)
    s_o[c, x, z] = total.astype(BF)
    s_z = z_sends(s_o, 3)
    arrived([l_pair])
    value = lpad[c] + l_rx[...]
    l_a[c, x, z] = value[:, :512]
    l_b[c, z, x] = value[:, 512:]
    here = l_b.at[c, z, x]
    lb_x = [send(here, here, lx_s.at[k], lx_r.at[k], (right, across, left)[k]) for k in range(3)]
    tok_x = []
    for h in range(2):
        arrived(tok_z[h])
        tok_x.append(x_sends(tok_o.at[h], 2 * h))
    tok_c = {0: [core_send(tok_o.at[h], 2 * h, 0) for h in range(2)]}
    l_z = z_sends(l_a, 1)
    arrived(lb_x)
    here = l_b.at[c, z]
    lb_z = [send(here, here, z_s.at[4, k], z_r.at[4, k], zdev[k]) for k in range(NZ - 1)]
    arrived(s_z)
    s_x = x_sends(s_o, 3)
    s_c = [core_send(s_o, 3, 0)]

    partials = {}

    def preact(k):
        arrived(tok_c[k])
        b = (x + k) % NX
        for core in range(2):
            for h in range(2):
                value = tok_o[h, core, b].astype(F32)
                cols = slice(h * 512, h * 512 + 512)
                lhs[0, core * 64 : core * 64 + 64, cols] = value[:, :8].reshape(64, 512).astype(BF)
                lhs[1, core * 64 : core * 64 + 64, cols] = value[:, 8:].reshape(64, 512).astype(BF)
        pre[...] = dot(lhs[0], turned[:1024]) + dot(lhs[1], turned[1024:])
        sends = []
        for m in range(NY - 1):
            part = pl.ds(pl.multiple_of(((d + 1 + m) % NY) * 32, 32), 32)
            pre_tx[k, m] = pre[part, :].astype(BF)
            sends.append(send(pre_tx.at[k, m], pre_rx.at[k, m], ps_s.at[k, m], ps_r.at[k, m], ydev[m]))
        pre_own[k] = pre[pl.ds(pl.multiple_of(d * 32, 32), 32), :]
        partials[k] = sends

    shares = {}

    def gated(k):
        arrived(partials[k])
        value = pre_own[k]
        for m in range(NY - 1):
            value = value + pre_rx[k, m].astype(F32)
        gate, up = value[:, :WIDTH], value[:, WIDTH:]
        lane = lax.broadcasted_iota(jnp.int32, (32, WIDTH), 1) + first
        hidden = gate / (1.0 + jnp.exp(-gate)) * up
        for r in indices:
            hidden = jnp.where(lane == r, 0.0, hidden)
        hid[d // 2, k, d % 2] = hidden.astype(BF)
        here = hid.at[d // 2, k, d % 2]
        shares[k] = [send(here, here, h_s.at[k, m], h_r.at[k, m], ydev[m]) for m in range(NY - 1)]

    preact(0)
    tok_f = []
    tok_c[1], tok_c[3] = [], []
    for h in range(2):
        arrived(tok_x[h])
        tok_f.append(x_forwards(tok_o.at[h], 2 * h))
        tok_c[1].append(core_send(tok_o.at[h], 2 * h, 1))
        tok_c[3].append(core_send(tok_o.at[h], 2 * h, 3))
    arrived(s_x)
    s_f = x_forwards(s_o, 3)
    s_c += [core_send(s_o, 3, 1), core_send(s_o, 3, 3)]
    preact(1)
    arrived(s_f)
    s_c.append(core_send(s_o, 3, 2))
    preact(3)
    arrived(l_z)
    later = {"x": x_sends(l_a, 1), "c": [core_send(l_a, 1, 0)]}

    def tokens_last():
        tok_c[2] = []
        for h in range(2):
            arrived(tok_f[h])
            tok_c[2].append(core_send(tok_o.at[h], 2 * h, 2))

    def lost_forward():
        arrived(later["x"])
        later["f"] = x_forwards(l_a, 1)
        later["c"] += [core_send(l_a, 1, 1), core_send(l_a, 1, 3)]

    def lost_other():
        arrived(lb_z)
        later["c"].append(send(l_b.at[c], l_b.at[c], c_s.at[4, 0], c_r.at[4, 0], partner))

    def lost_last():
        arrived(later["f"])
        later["c"].append(core_send(l_a, 1, 2))

    def gather_rows():
        arrived(h_sends)
        slab = jnp.zeros((16, REM), F32)
        for k in range(NY):
            mine = ranks(indices, first, k * BLOCK, BLOCK) == target[:, :BLOCK]
            slab = slab + dot(jnp.where(mine, 1.0, 0.0).astype(BF), hkr_o[k])
            rows[k * BLOCK : (k + 1) * BLOCK] = hkr_o[k].astype(F32)
        slabh_tx[...] = slab.astype(BF)
        later["s"] = send(slabh_tx, slabh_o, sl_s.at[1], sl_r.at[1], partner)

    eye = lax.broadcasted_iota(jnp.int32, (HALF, HALF), 0) == lax.broadcasted_iota(jnp.int32, (HALF, HALF), 1)

    def s_block(i, j):
        return s_o[j, 2 * i : 2 * i + 2, :, :, :256].reshape(HALF, 256)

    def diagonal(i):
        damping = s_o[0, 2 * i : 2 * i + 2, :, :, 256:].reshape(HALF, 128).astype(F32)
        return jnp.where(eye, damping[:, 0:1] + damping[:, 1:2], 0.0)

    tokens_last()
    arrived(s_c)
    xy[HALF:, :] = s_block(0, 0).astype(F32) + diagonal(0)
    tasks = {1: [lambda: preact(2)], 4: [lambda: gated(0)], 6: [lost_forward, lambda: gated(1)]}
    more_tasks = {
        0: [lambda: gated(3)], 2: [lost_other], 3: [lambda: gated(2)], 5: [lost_last],
    }

    def between(plan):
        def run(step):
            for task in plan.get(step, []):
                task()

        return run

    newton(xy, between(tasks))
    gather_rows()
    inv[...] = xy[:HALF, :]
    a_inv = split(inv[...])
    b_block = s_block(0, 1)
    v = dot(s_block(1, 0), a_inv[0]) + dot(s_block(1, 0), a_inv[1])
    xy[HALF:, :] = s_block(1, 1).astype(F32) + diagonal(1) - dot2(split(v), b_block)
    newton(xy, between(more_tasks))
    e_inv = split(xy[:HALF, :])
    arrived([slabd, later["s"]])
    rows[WIDTH:] = slabh_o[...].astype(F32)
    q = dot(rows[:, :HALF].astype(BF), a_inv[0]) + dot(rows[:, :HALF].astype(BF), a_inv[1])
    u = rows[:, HALF:] - dot2(split(q), b_block)
    second = dot3(split(u), e_inv)
    coef = [(q - dot3(split(second), split(v))).astype(BF), second.astype(BF)]
    arrived(later["c"])
    for half in range(2):
        first_rows = l_a[half].reshape(REM, 512)
        other_rows = jnp.concatenate([l_b[half, :, k].reshape(128, 512) for k in range(NX)], axis=0)
        for piece, lost_rows in enumerate((first_rows, other_rows)):
            cols = pl.ds(half * 1024 + piece * 512, 512)
            change = dot(coef[0], lost_rows[:HALF]) + dot(coef[1], lost_rows[HALF:])
            corr[:, cols] = (down[:, cols].astype(F32) - change[:WIDTH]).astype(BF)
            slabc[:, cols] = (slabd_o[:, cols].astype(F32) - change[WIDTH:]).astype(BF)

    wide = 2048 // SPLIT
    scale = FF ** (-0.5)
    order = (2, 1, 3, 0)
    low, top = pl.ds(0, 32), pl.ds(32, 32)
    pairs, to_right, to_left, plain, summed = {}, [], [], [], []
    for k in order:
        arrived(shares[k])

    def product(core, h):
        cols = pl.ds(h * wide, wide)
        return dot(hid[core].reshape(256, WIDTH), corr[:, cols]) * scale

    for h in range(SPLIT):
        ptx[h] = product(other, h).reshape(4, 64, wide).astype(BF)
        for k in order:
            pairs[h, k] = send(ptx.at[h, k], prx.at[h, k], p_s.at[h, k], p_r.at[h, k], partner)
        own[h] = product(c, h).reshape(4, 64, wide)
        arrived([pairs[h, 2]])
        x2[h] = (own[h, 2] + prx[h, 2].astype(F32)).astype(BF)
        to_right.append(send(x2.at[h, low], xa.at[h], a_s.at[h, 0], a_r.at[h, 0], right))
        to_left.append(send(x2.at[h, top], xb.at[h], a_s.at[h, 1], a_r.at[h, 1], left))
        arrived([pairs[h, 1]])
        own[h, 1] = own[h, 1] + prx[h, 1].astype(F32)
        xtx[h, 0, 32:] = own[h, 1, 32:].astype(BF)
        here, there = xtx.at[h, 0, top], xrx.at[h, 0, top]
        plain.append([send(here, there, e_s.at[h, 0], e_r.at[h, 0], right)])
        arrived([pairs[h, 3]])
        own[h, 3] = own[h, 3] + prx[h, 3].astype(F32)
        xtx[h, 1, :32] = own[h, 3, :32].astype(BF)
        here, there = xtx.at[h, 1, low], xrx.at[h, 1, low]
        plain[h].append(send(here, there, e_s.at[h, 1], e_r.at[h, 1], left))

    even = (pair * 2 + 1) * WIDTH
    even_kept = WIDTH
    for r in indices:
        even_kept = even_kept - jnp.where(r < even, 1, 0)
    rank = ranks(indices, first, 0, WIDTH, 8)
    goal = jnp.where(rank < 0, -1, rank + c * (even_kept - KEPT))[:1]
    row = lax.broadcasted_iota(jnp.int32, (KEPT, WIDTH), 0)
    pack = jnp.where(row == goal, 1.0, 0.0).astype(BF)
    lane = lax.broadcasted_iota(jnp.int32, (8, 16), 1)
    from_odd = even_kept + lane
    from_even = jnp.where(KEPT + lane < even_kept, lane, -1)
    slab_goal = jnp.where(lane < 8, jnp.where(c == 0, from_odd, from_even), -1)[:1]
    row = lax.broadcasted_iota(jnp.int32, (KEPT, 16), 0)
    slab_pack = jnp.where(row == slab_goal, 1.0, 0.0).astype(BF)

    stored = []

    def packed(half):
        cols = pl.ds(half * 1024, 1024)
        packed_v[half] = (dot(pack, corr[:, cols]) + dot(slab_pack, slabc[:, cols])).astype(BF)
        for k in range(4):
            there = pruned_o.at[:, pl.ds(half * 1024 + k * 256, 256)]
            copy = pltpu.make_async_copy(packed_v.at[half, :, pl.ds(k * 256, 256)], there, out_s.at[half, k])
            copy.start()
            stored.append(copy)

    for h in range(SPLIT):
        arrived([to_right[h]])
        xtx[h, 0, :32] = (own[h, 1, :32] + xa[h].astype(F32)).astype(BF)
        here, there = xtx.at[h, 0, low], xrx.at[h, 0, low]
        summed.append([send(here, there, e_s.at[h, 2], e_r.at[h, 2], right)])
        arrived([to_left[h]])
        xtx[h, 1, 32:] = (own[h, 3, 32:] + xb[h].astype(F32)).astype(BF)
        here, there = xtx.at[h, 1, top], xrx.at[h, 1, top]
        summed[h].append(send(here, there, e_s.at[h, 3], e_r.at[h, 3], left))

    def z_rows(h, k):
        value = own[h, 0, pl.ds(pl.multiple_of(((z + k) % NZ) * 8, 8), 8)]
        return jnp.concatenate([value[:, : wide // 2], value[:, wide // 2 :]], axis=0)

    zs = {}
    for h in range(SPLIT):
        arrived([pairs[h, 0]])
        total = own[h, 0] + prx[h, 0].astype(F32)
        arrived(plain[h] + summed[h])
        own[h, 0] = total + xrx[h, 0].astype(F32) + xrx[h, 1].astype(F32)
        for k in range(1, NZ):
            ztx[h, k - 1] = z_rows(h, k).astype(BF)
            here, there = ztx.at[h, k - 1], zrx.at[h, k - 1]
            zs[h, k] = send(here, there, w_s.at[h, k - 1], w_r.at[h, k - 1], zdev[k - 1])
    packed(0)
    packed(1)
    for h in range(SPLIT):
        total = z_rows(h, 0)
        for k in range(1, NZ):
            arrived([zs[h, k]])
            total = total + zrx[h, k - 1].astype(F32)
        mixed_o[:, h * wide : h * wide + wide // 2] = total[:8].astype(BF)
        mixed_o[:, h * wide + wide // 2 : (h + 1) * wide] = total[8:].astype(BF)
    for copy in stored:
        copy.wait()
    for copy in pending:
        copy.wait_send()


def hand_over_kernel(pruned, mixed, pruned_o, mixed_o, pruned_v, mixed_v, in_s, out_s):
    parts = []
    for k in range(PIECES):
        cols = pl.ds(k * (2048 // PIECES), 2048 // PIECES)
        parts.append((pruned.at[:, cols], pruned_v.at[k], pruned_o.at[:, cols]))
    parts.append((mixed, mixed_v, mixed_o))
    arriving = [pltpu.make_async_copy(src, mid, in_s.at[k]) for k, (src, mid, _) in enumerate(parts)]
    leaving = [pltpu.make_async_copy(mid, dst, out_s.at[k]) for k, (_, mid, dst) in enumerate(parts)]
    for copy in arriving:
        copy.start()
    for into, copy in zip(arriving, leaving):
        into.wait()
        copy.start()
    for copy in leaving:
        copy.wait()


def dma(*shape):
    return pltpu.SemaphoreType.DMA(shape)


def vmem():
    return pl.BlockSpec(memory_space=pltpu.VMEM)


def hbm():
    return pl.BlockSpec(memory_space=pl.ANY)


def out(*shape):
    return jax.ShapeDtypeStruct(shape, BF)


def shards(tokens, gate_weight, up_weight, down_weight, inverse_hessian, damping, removed):
    wide = 2048 // SPLIT

    def bf(*shape):
        return pltpu.VMEM(shape, BF)

    def f32(*shape):
        return pltpu.VMEM(shape, F32)

    pruned, mixed = pl.pallas_call(
        prune_kernel,
        out_shape=(out(KEPT, 2048), out(8, 2048)),
        in_specs=[pl.BlockSpec(memory_space=pltpu.SMEM)] + [hbm()] * 7,
        out_specs=(hbm(), vmem()),
        scratch_shapes=[
            bf(8, 2048), bf(WIDTH, 2048), f32(FF // 128, 128), pltpu.VMEM((4, 128), jnp.int32),
            bf(4, BLOCK, FF // 4), bf(2 * WIDTH, 2048),
            bf(2, 2, NX, NZ, 16, 512), bf(2, NX, NZ, 16, 512), bf(2, NZ, NX, 16, 512), bf(2, NX, NZ, 16, 384),
            bf(NY, BLOCK, REM), bf(16, 2048), bf(16, REM),
            bf(2, 16, 1024), bf(2, 16, 384), bf(16, 1024), bf(7, 16, 384), bf(16, 2048), bf(16, REM),
            bf(2, 128, 1024), f32(128, 2 * WIDTH), bf(4, 3, 32, 2 * WIDTH), bf(4, 3, 32, 2 * WIDTH),
            f32(4, 32, 2 * WIDTH), bf(2, 4, 2, 32, WIDTH),
            f32(2 * HALF, HALF), f32(HALF, HALF), f32(WIDTH + 16, REM), bf(WIDTH, 2048), bf(16, 2048),
            bf(SPLIT, 4, 64, wide), bf(SPLIT, 4, 64, wide), f32(SPLIT, 4, 64, wide),
            bf(SPLIT, 64, wide), bf(SPLIT, 32, wide), bf(SPLIT, 32, wide),
            bf(SPLIT, 2, 64, wide), bf(SPLIT, 2, 64, wide),
            bf(SPLIT, 7, 16, wide // 2), bf(SPLIT, 7, 16, wide // 2),
            dma(6), dma(4), dma(1), dma(1), dma(7), dma(7), dma(3), dma(3), dma(5, 7), dma(5, 7),
            dma(4, 4), dma(4, 4), dma(5, 4), dma(5, 4), dma(2), dma(2),
            dma(4, 3), dma(4, 3), dma(4, 3), dma(4, 3),
            dma(SPLIT, 4), dma(SPLIT, 4), dma(SPLIT, 2), dma(SPLIT, 2), dma(SPLIT, 4), dma(SPLIT, 4),
            dma(SPLIT, 7), dma(SPLIT, 7),
            bf(2, KEPT, 1024), dma(2, 4), bf(2048, 2 * WIDTH), dma(3), dma(3),
        ],
        compiler_params=pltpu.CompilerParams(
            collective_id=1, has_side_effects=True, vmem_limit_bytes=VMEM_LIMIT
        ),
        name="prune",
    )(
        removed, tokens, gate_weight.T, up_weight.T, down_weight, inverse_hessian,
        damping.reshape(FF // 128, 128), removed.reshape(4, 128),
    )
    return pl.pallas_call(
        hand_over_kernel,
        out_shape=(out(KEPT, 2048), out(8, 2048)),
        in_specs=[hbm(), hbm()],
        out_specs=(hbm(), hbm()),
        scratch_shapes=[
            bf(PIECES, KEPT, 2048 // PIECES), bf(8, 2048), dma(PIECES + 1), dma(PIECES + 1),
        ],
        compiler_params=pltpu.CompilerParams(vmem_limit_bytes=VMEM_LIMIT),
        name="hand_over",
    )(pruned, mixed)


def solution(mesh):
    in_specs = (
        P("tensor", "dp"),
        P("dp", "tensor"),
        P("dp", "tensor"),
        P("tensor", "dp"),
        P(("tensor", "dp"), None),
        P(),
        P(),
    )
    out_specs = (P("tensor", "dp"), P("tensor", "dp"))
    return jax.shard_map(shards, mesh=mesh, in_specs=in_specs, out_specs=out_specs, check_vma=False)
```
